128 devices in a mesh: dp: 32 (over x, z, y_hi), seq: 4 (over y_lo, core).
Axes of the slice: x: 4, y: 4 (y_hi: 2, y_lo: 2; y = y_hi * 2 + y_lo), z: 4, core: 2. Of those that a mesh axis runs over, the one named last changes fastest.
Arguments:
- query_proj: bfloat16 [32768, 2560], P(('dp', 'seq')), may hold values from -80 to 80
- key_proj: bfloat16 [32768, 2560], P(('dp', 'seq')), may hold values from -4 to 4
- value_proj: bfloat16 [32768, 2560], P(('dp', 'seq')), may hold values from -5 to 5
- cotangent: bfloat16 [32768, 2560], P(('dp', 'seq')), may hold values from -48 to 48
- out_weight: bfloat16 [2560, 2560], P('seq'), may hold values from -0.125 to 0.125
- tile_list: int32 [8, 6], replicated, may hold values from 0 to 7, as said below
- owners: int32 [400, 1], replicated, may hold values from 0 to 31; in each aligned block of 100 rows (0 to 99, 100 to 199, ...) at most 7 rows name the same one
- master: float32 [32, 28, 128, 128], P('dp', 'seq'), may hold values from -0.3 to 0.3
- moment_one: float32 [32, 28, 128, 128], P('dp', 'seq'), may hold values from -24 to 24
- moment_two: float32 [32, 28, 128, 128], P('dp', 'seq'), may hold values from 10 to 1000
- average: float32 [32, 28, 128, 128], P('dp', 'seq'), may hold values from -0.3 to 0.3
Outputs:
- query_grad: bfloat16 [32768, 2560], P(('dp', 'seq'))
- key_grad: bfloat16 [32768, 2560], P(('dp', 'seq'))
- value_grad: bfloat16 [32768, 2560], P(('dp', 'seq'))
- new_weight: bfloat16 [2560, 2560], P('seq')
- new_master: float32 [32, 28, 128, 128], P('dp', 'seq')
- new_moment_one: float32 [32, 28, 128, 128], P('dp', 'seq')
- new_moment_two: float32 [32, 28, 128, 128], P('dp', 'seq')
- new_average: float32 [32, 28, 128, 128], P('dp', 'seq')
The draws below stay inside these ranges and needn't reach their ends.
Inputs may be any that keep to these rules, and one draw needn't show every extreme that they name: `tile_list`: row i lists 6 different key tiles, the first being i itself. `owners`: among the 100 blocks of one group no data index owns more than 7, and in some group one owns exactly 7.
All inputs are finite; a program needn't handle non-finite values.
Results may differ from the reference program's by a relative error of at most 0.0085.
Values may be sent and summed in bfloat16 or wider, within the bound.
A program may use at most 320 MiB of HBM per device.

```python
import math
import jax
import jax.numpy as jnp
import numpy as np
from jax import lax

HEADS = 20
HS = 128
OUTW = 2560
KT = 6
CT = 128
LENGTH = 1024
TOKENS = 32768
NTILE = 8
NCB = 20
BLOCKS_DEV = 100
BLOCKS = 400
SLOTS = 7
N_DP = 32
N_SEQ = 4


def draw_key_proj(key, part):
    key = jax.random.fold_in(key, 7)
    result = jnp.clip(jax.random.normal(key, (TOKENS, HEADS * HS), jnp.float32), -4.0, 4.0)
    return result.astype(jnp.bfloat16)


def draw_query_proj(key, part):
    key = jax.random.fold_in(key, 3)
    own_draw = jnp.clip(jax.random.normal(jax.random.fold_in(key, 1), (TOKENS, HEADS * HS), jnp.float32), -4.0, 4.0)
    result = own_draw
    return result.astype(jnp.bfloat16)


def draw_tile_list(key, part):
    key = jax.random.fold_in(key, 5)
    tile_keys = jax.random.split(key, NTILE)
    shuffled = jax.vmap(lambda subkey: jax.random.permutation(subkey, NTILE - 1))(tile_keys) + 1
    tile_rows = jnp.arange(NTILE, dtype=jnp.int32)[:, None]
    others = (tile_rows + shuffled[:, :KT - 1].astype(jnp.int32)) % NTILE
    return jnp.concatenate([tile_rows, others], axis=1).astype(jnp.int32)


def block_scale(stream_key, shape, cuts, least, high):
    def one(dim, shards_of):
        draws = jax.random.uniform(jax.random.fold_in(jax.random.fold_in(stream_key, 6), dim), (shards_of,), jnp.float32, least / len(cuts), high / len(cuts))
        return jnp.repeat(jnp.exp(draws), shape[dim] // shards_of).reshape((-1,) + (1,) * (len(shape) - dim - 1))

    factor_of = one(*cuts[0])
    for cut in cuts[1:]:
        factor_of = factor_of * one(*cut)
    return factor_of


def shared_out(rng, own, number, rows, number_of, top, bound, skew):
    sequence = jax.random.permutation(rng, number_of)
    crowded, usual = load_shares(number_of, rows * top, bound, skew, True), load_shares(number_of, rows * top, bound, skew, False)
    places = jnp.arange(number_of)

    def named(sizes, turn):
        used = int((sizes > 0).sum())
        fixed = max(1, used // 4)
        passed = fixed + (places - fixed + turn * (used - fixed)) % max(1, number_of - fixed)
        return jnp.zeros((number_of,), jnp.int32).at[sequence[jnp.where(places < fixed, places, passed)]].set(jnp.asarray(sizes, jnp.int32))

    sizes = jnp.where(number % 4 == 0, named(crowded, number // 4), named(usual, number - number // 4 - 1))
    mixed = jax.random.permutation(jax.random.fold_in(own, 3), number_of)
    donor, receiver = mixed[0:number_of // 2 * 2:2], mixed[1:number_of // 2 * 2:2]
    room = jnp.minimum(sizes[donor] - 1, bound - sizes[receiver]) // 2
    room = jnp.where((donor == sequence[0]) | (receiver == sequence[0]) | (sizes[receiver] == 0), 0, jnp.maximum(room, 0))
    passed = jax.random.randint(jax.random.fold_in(own, 4), (number_of // 2,), 0, 1 << 20) % (room + 1)
    sizes = sizes.at[donor].add(-passed).at[receiver].add(passed)
    labels = jnp.searchsorted(jnp.cumsum(sizes), jnp.arange(rows * top), side="right").astype(jnp.int32)
    table = labels.reshape(top, rows).T
    table = table[jax.random.permutation(jax.random.fold_in(own, 1), rows)]
    turn = jax.random.randint(jax.random.fold_in(own, 2), (rows, 1), 0, top)
    return jnp.take_along_axis(table, (jnp.arange(top)[None, :] + turn) % top, axis=1)


def load_shares(amount, total, most, slope, full):
    weights = [(1 << 20) // math.isqrt(grade ** slope) + 1 for grade in range(1, amount + 1)]
    largest = most if full else min(most, max(-(-total // amount), total * weights[0] // sum(weights)))
    least = 1 if total - largest >= amount - 1 else 0
    holding, spare = [largest] + [least] * (amount - 1), total - largest - least * (amount - 1)
    while spare > 0:
        candidates = [i for i in range(1, amount) if holding[i] < largest] or [i for i in range(1, amount) if holding[i] < most]
        pool, left = sum([weights[i] for i in candidates]), spare
        for i in candidates:
            more = min(most - holding[i], max(1, left * weights[i] // pool), spare)
            holding[i] = holding[i] + more
            spare = spare - more
    return np.array(holding)


def normal_values(stream_key, shape, deviation, most, cuts=(), held_as=jnp.bfloat16):
    entries = deviation * jax.random.normal(stream_key, shape, jnp.float32)
    if cuts:
        entries = entries * block_scale(stream_key, shape, cuts, -0.22, 0.18)
    return jnp.clip(entries, -most, most).astype(held_as)


def setup_inputs(seed: int = 0) -> dict:
    streams_of = jax.random.split(jax.random.key(seed), 12)
    query_proj = draw_query_proj(jax.random.fold_in(streams_of[11], 71), 0)
    key_proj = draw_key_proj(jax.random.fold_in(streams_of[11], 71), 0)
    value_proj = normal_values(streams_of[2], (TOKENS, HEADS * HS), 1.0, 5.0, ((0, 128),))
    cotangent = normal_values(streams_of[3], (TOKENS, OUTW), 8.0, 48.0, ((0, 128),))
    out_weight = normal_values(streams_of[4], (HEADS * HS, OUTW), (HEADS * HS) ** -0.5, 0.125, ((0, 4),))
    tile_list = draw_tile_list(jax.random.fold_in(streams_of[11], 71), 0)
    owners_keys = jax.random.split(jax.random.fold_in(streams_of[6], 1), BLOCKS // BLOCKS_DEV)
    owners_turns = jax.random.permutation(jax.random.fold_in(streams_of[6], 3), BLOCKS // BLOCKS_DEV)
    owners = jax.vmap(lambda own, number: shared_out(jax.random.fold_in(streams_of[6], 2), own, number, BLOCKS_DEV, N_DP, 1, SLOTS, 2))(owners_keys, owners_turns).reshape((BLOCKS, 1))
    master = normal_values(streams_of[7], (N_DP, N_SEQ * SLOTS, HS, CT), 0.05, 0.3, ((0, 32), (1, 4)), jnp.float32)
    moment_one = normal_values(streams_of[8], (N_DP, N_SEQ * SLOTS, HS, CT), 4.0, 24.0, ((0, 32), (1, 4)), jnp.float32)
    moment_two = jnp.clip(jnp.exp(math.log(1000.0) - 4.6051702 * jax.random.uniform(streams_of[9], (N_DP, N_SEQ * SLOTS, HS, CT), jnp.float32) ** block_scale(streams_of[9], (N_DP, N_SEQ * SLOTS, HS, CT), ((0, 32), (1, 4)), -0.2, 0.2)), 10.0, 1000.0)
    average = normal_values(streams_of[10], (N_DP, N_SEQ * SLOTS, HS, CT), 0.05, 0.3, ((0, 32), (1, 4)), jnp.float32)
    return {"query_proj": query_proj, "key_proj": key_proj, "value_proj": value_proj, "cotangent": cotangent, "out_weight": out_weight, "tile_list": tile_list, "owners": owners, "master": master, "moment_one": moment_one, "moment_two": moment_two, "average": average}


learn_rate = 0.001
beta_one = 0.9
beta_two = 0.95
adam_eps = 1e-08
weight_decay = 0.1
ema_keep = 0.99
bias_one = 1.0 - (0.9 ** 50) ** 2
bias_two = 1.0 - (0.95 ** 50) ** 2

def round_keep(values):
    return lax.optimization_barrier(values.astype(jnp.bfloat16)).astype(jnp.float32)

def block_attention(query, keyed, valued, d_attn, tile_list):
    length, head_count, head_width = query.shape
    tile_count, kcount = tile_list.shape
    tile_len = length // tile_count
    score_scale = 1.0 / math.sqrt(head_width)
    high = lax.Precision.HIGHEST
    query_t = query.reshape(tile_count, tile_len, head_count, head_width).astype(jnp.float32)
    key_sel = keyed.reshape(tile_count, tile_len, head_count, head_width)[tile_list]
    key_sel = key_sel.reshape(tile_count, kcount * tile_len, head_count, head_width).astype(jnp.float32)
    value_sel = valued.reshape(tile_count, tile_len, head_count, head_width)[tile_list]
    value_sel = value_sel.reshape(tile_count, kcount * tile_len, head_count, head_width).astype(jnp.float32)
    d_tiles = d_attn.reshape(tile_count, tile_len, head_count, head_width).astype(jnp.float32)
    scores = jnp.einsum('iqhd,ikhd->ihqk', query_t, key_sel, precision=high) * score_scale
    row_top = lax.optimization_barrier(jnp.max(scores, axis=-1, keepdims=True))
    exp_scores = jnp.exp(scores - row_top)
    softmax_f = exp_scores / lax.optimization_barrier(jnp.sum(exp_scores, axis=-1, keepdims=True))
    softmax_b = round_keep(softmax_f)
    attention = jnp.einsum('ihqk,ikhd->iqhd', softmax_b, value_sel, precision=high).astype(jnp.bfloat16)
    d_prob = jnp.einsum('iqhd,ikhd->ihqk', d_tiles, value_sel, precision=high)
    row_delta = lax.optimization_barrier(jnp.sum(softmax_f * d_prob, axis=-1, keepdims=True))
    d_score = round_keep(softmax_f * (d_prob - row_delta) * score_scale)
    query_grad = jnp.einsum('ihqk,ikhd->iqhd', d_score, key_sel, precision=high).astype(jnp.bfloat16)
    key_part = jnp.einsum('ihqk,iqhd->ikhd', d_score, query_t, precision=high)
    value_part = jnp.einsum('ihqk,iqhd->ikhd', softmax_b, d_tiles, precision=high)
    key_part = key_part.reshape(tile_count, kcount, tile_len * head_count * head_width)
    value_part = value_part.reshape(tile_count, kcount, tile_len * head_count * head_width)
    tile_ids = jnp.arange(tile_count, dtype=jnp.int32)
    onehot = (tile_list[:, :, None] == tile_ids[None, None, :]).astype(jnp.float32)
    key_grad = jnp.einsum('ijn,ijc->nc', onehot, key_part, precision=high).astype(jnp.bfloat16)
    value_grad = jnp.einsum('ijn,ijc->nc', onehot, value_part, precision=high).astype(jnp.bfloat16)
    flat = (length, head_count * head_width)
    return (attention.reshape(flat), query_grad.reshape(flat), key_grad.reshape(flat), value_grad.reshape(flat))

def adam_step(master_in, first_in, second_in, mean_in, gradient):
    first_out = beta_one * first_in + (1.0 - beta_one) * gradient
    second_out = beta_two * second_in + (1.0 - beta_two) * gradient * gradient
    direction = first_out / bias_one / (jnp.sqrt(second_out / bias_two) + adam_eps)
    master_out = master_in - learn_rate * (direction + weight_decay * master_in)
    mean_out = ema_keep * mean_in + (1.0 - ema_keep) * master_out
    return (master_out, first_out, second_out, mean_out)

def reference(query_proj, key_proj, value_proj, cotangent, out_weight, tile_list, owners, master, moment_one, moment_two, average):
    head_total = HEADS * HS

    def replica(grad_sum, replica_index):
        offset = (replica_index * LENGTH).astype(jnp.int32)
        query = lax.dynamic_slice_in_dim(query_proj, offset, LENGTH, 0).reshape(LENGTH, HEADS, HS)
        keyed = lax.dynamic_slice_in_dim(key_proj, offset, LENGTH, 0).reshape(LENGTH, HEADS, HS)
        valued = lax.dynamic_slice_in_dim(value_proj, offset, LENGTH, 0).reshape(LENGTH, HEADS, HS)
        upstream = lax.dynamic_slice_in_dim(cotangent, offset, LENGTH, 0)
        d_attn = jnp.dot(upstream, out_weight.T, preferred_element_type=jnp.float32).astype(jnp.bfloat16)
        attention, query_grad, key_grad, value_grad = block_attention(query, keyed, valued, d_attn.reshape(LENGTH, HEADS, HS), tile_list)
        grad_sum = grad_sum + jnp.dot(attention.T, upstream, preferred_element_type=jnp.float32)
        return (grad_sum, (query_grad, key_grad, value_grad))
    start_grad = jnp.zeros((head_total, OUTW), jnp.float32)
    grad_sum, grads = lax.scan(replica, start_grad, jnp.arange(N_DP, dtype=jnp.int32))
    query_grad = grads[0].reshape(TOKENS, head_total)
    key_grad = grads[1].reshape(TOKENS, head_total)
    value_grad = grads[2].reshape(TOKENS, head_total)
    weight_grad = grad_sum / N_DP
    block_grad = weight_grad.reshape(HEADS, HS, NCB, CT).transpose(0, 2, 1, 3).reshape(BLOCKS, HS, CT)
    owner_ids = owners[:, 0].astype(jnp.int32)
    block_ids = jnp.arange(BLOCKS, dtype=jnp.int32)
    group_ids = block_ids // BLOCKS_DEV
    earlier = (owner_ids[:, None] == owner_ids[None, :]) & (group_ids[:, None] == group_ids[None, :]) & (block_ids[None, :] < block_ids[:, None])
    slot_of = lax.optimization_barrier(jnp.sum(earlier.astype(jnp.int32), axis=1)).astype(jnp.int32)
    column = (group_ids * SLOTS + slot_of).astype(jnp.int32)
    grad_state = jnp.zeros_like(master).at[owner_ids, column].set(block_grad)
    filled = jnp.zeros(master.shape[:2], jnp.float32).at[owner_ids, column].set(1.0) > 0.5
    stepped = adam_step(master, moment_one, moment_two, average, grad_state)
    keep = filled[:, :, None, None]
    new_master = jnp.where(keep, stepped[0], master)
    new_moment_one = jnp.where(keep, stepped[1], moment_one)
    new_moment_two = jnp.where(keep, stepped[2], moment_two)
    new_average = jnp.where(keep, stepped[3], average)
    blocks_new = new_master[owner_ids, column].astype(jnp.bfloat16)
    new_weight = blocks_new.reshape(HEADS, NCB, HS, CT).transpose(0, 2, 1, 3).reshape(head_total, OUTW)
    return (query_grad, key_grad, value_grad, new_weight, new_master, new_moment_one, new_moment_two, new_average)
```

```python
import math

import jax
import jax.numpy as jnp
from jax import lax
from jax.experimental import pallas as pl
from jax.experimental.pallas import tpu as pltpu
from jax.sharding import PartitionSpec as P

MESH = pl.DeviceIdType.MESH
BF = jnp.bfloat16
F32 = jnp.float32

learn_rate = 0.001
beta_one = 0.9
beta_two = 0.95
adam_eps = 1e-08
weight_decay = 0.1
ema_keep = 0.99
bias_one = 1.0 - (0.9**50) ** 2
bias_two = 1.0 - (0.95**50) ** 2

HD = 5
TOK = 256
LEN = 1024
OUTW = 2560
SL = 7
NEG = -1e30
SCALE = 1.0 / math.sqrt(128.0)
SCALE2 = SCALE * math.log2(math.e)
CC = 4


def aligned(value, step):
    return pl.multiple_of(value * step, step)


def remote(src, dst, send, recv, device):
    return pltpu.make_async_remote_copy(
        src_ref=src, dst_ref=dst, send_sem=send, recv_sem=recv, device_id=device, device_id_type=MESH
    )


def dot(a, b):
    return lax.dot_general(a, b, (((1,), (0,)), ((), ())), preferred_element_type=F32)


def dot_nt(a, b):
    return lax.dot_general(a, b, (((1,), (1,)), ((), ())), preferred_element_type=F32)


def place_of():
    dp = lax.axis_index("dp")
    return dp, lax.axis_index("seq"), dp // 8, (dp // 2) % 4, dp % 2


def dp_index(x, z, yh):
    return (x * 4 + z) * 2 + yh


def ring(value, step):
    return lax.rem(value + step, 4)


def attend_kernel(
    q_in, k_in, v_in, cot_in, w_in, bias,
    dq_out, dk_out, dv_out, rs_out,
    qkv, cot, w, da, back, kt, vt, att, dk_acc, dv_acc,
    gx, gz, r1x, r1z, s2x, s2z, r2x, r2z, s3, k3, r3,
    local_sem, back_local, cot_send, cot_recv, in_send, in_recv, back_send, back_recv,
    x1_send, x1_recv, z1_send, z1_recv, x2_send, x2_recv, z2_send, z2_recv, y_send, y_recv,
):
    dp, me, x, z, yh = place_of()
    sibling = me + 1 - 2 * lax.rem(me, 2)
    across = ring(me, 2)
    corner = ring(sibling, 2)
    peers = [ring(me, p) for p in (1, 2, 3)]
    sources = [ring(me, 4 - p) for p in (1, 2, 3)]
    inputs = (q_in, k_in, v_in)
    outputs = (dq_out, dk_out, dv_out)

    barrier = pltpu.get_barrier_semaphore()
    for t in peers:
        pl.semaphore_signal(barrier, inc=1, device_id=(dp, t), device_id_type=MESH)
    for p in (1, 2, 3):
        pl.semaphore_signal(barrier, inc=1, device_id=(dp_index(ring(x, p), z, yh), me), device_id_type=MESH)
        pl.semaphore_signal(barrier, inc=1, device_id=(dp_index(x, ring(z, p), yh), me), device_id_type=MESH)
    pl.semaphore_signal(barrier, inc=1, device_id=(dp_index(x, z, 1 - yh), me), device_id_type=MESH)
    pl.semaphore_wait(barrier, 10)

    def rows(s, n=TOK):
        return pl.ds(aligned(s, TOK), n)

    def cot_rows(s, c):
        return pl.ds(pl.multiple_of(s * TOK + c * (TOK // CC), TOK // CC), TOK // CC)

    def cot_cross(c):
        return remote(
            cot_in.at[pl.ds(c * (TOK // CC), TOK // CC)], cot.at[cot_rows(me, c)],
            cot_send.at[c], cot_recv.at[c], (dp, across),
        )

    def cot_sibling():
        return remote(cot_in, cot.at[rows(me)], cot_send.at[CC], cot_recv.at[CC], (dp, sibling))

    def cot_forward(c):
        part = cot.at[cot_rows(across, c)]
        return remote(part, part, cot_send.at[CC + 1 + c], cot_recv.at[CC + 1 + c], (dp, sibling))

    def cot_own():
        return pltpu.make_async_copy(cot_in, cot.at[rows(me)], local_sem.at[0])

    def w_own():
        return pltpu.make_async_copy(w_in, w, local_sem.at[1])

    def head_columns(t, h):
        return pl.ds(pl.multiple_of((t * HD + h) * 128, 128), 128)

    def head_send(h, a, p):
        t = peers[p]
        return remote(
            inputs[a].at[:, head_columns(t, h)], qkv.at[a, h, rows(me)],
            in_send.at[h, a, p], in_recv.at[h, a, p], (dp, t),
        )

    def head_recv(h, a, p):
        part = qkv.at[a, h, rows(sources[p])]
        return remote(part, part, in_send.at[h, a, p], in_recv.at[h, a, p], (dp, sources[p]))

    def head_own(h, a):
        return pltpu.make_async_copy(
            inputs[a].at[:, head_columns(me, h)], qkv.at[a, h, rows(me)], local_sem.at[2 + 3 * h + a]
        )

    def back_copy(h, a, p):
        t = peers[p]
        return remote(
            back.at[a, h, rows(t)], outputs[a].at[:, head_columns(me, h)],
            back_send.at[h, a, p], back_recv.at[h, a, p], (dp, t),
        )

    def back_recv_copy(h, a, p):
        return remote(
            back.at[a, h, rows(sources[p])], outputs[a].at[:, head_columns(sources[p], h)],
            back_send.at[h, a, p], back_recv.at[h, a, p], (dp, sources[p]),
        )

    def back_own(h, a):
        return pltpu.make_async_copy(
            back.at[a, h, rows(me)], outputs[a].at[:, head_columns(me, h)], back_local.at[h, a]
        )

    cot_own().start()
    w_own().start()
    for c in range(CC):
        cot_cross(c).start()
    cot_sibling().start()

    @pl.loop(0, HD)
    def _(h):
        for a in range(3):
            head_own(h, a).start()
            for p in range(3):
                head_send(h, a, p).start()

    for c in range(CC):
        cot_cross(c).wait_recv()
        cot_forward(c).start()
    cot_own().wait()
    w_own().wait()
    cot_sibling().wait_recv()
    for c in range(CC):
        cot_forward(c).wait_recv()

    @pl.loop(0, 4)
    def _(b):
        d_rows = dot_nt(cot[pl.ds(aligned(b, 256), 256), :], w[...]).astype(BF)
        for h in range(HD):
            da[h, pl.ds(aligned(b, 256), 256), :] = d_rows[:, h * 128 : (h + 1) * 128]

    def compute(h):
        kt[...] = qkv[1, h].T
        vt[...] = qkv[2, h].T
        dk_acc[...] = jnp.zeros_like(dk_acc)
        dv_acc[...] = jnp.zeros_like(dv_acc)

        @pl.loop(0, 4)
        def _(b):
            part = pl.ds(aligned(b, 256), 256)
            q_b = qkv[0, h, part, :]
            da_b = da[h, part, :]
            score = dot_nt(qkv[1, h], q_b).reshape(8, 128, 256) * SCALE2 + bias[b][:, None, :]
            score = score.reshape(LEN, 256)
            top = jnp.max(score, axis=0, keepdims=True)
            weight = jnp.exp2(score - top)
            total = jnp.sum(weight, axis=0, keepdims=True)
            prob = weight * (1.0 / total)
            prob_b = prob.astype(BF)
            d_prob = dot_nt(qkv[2, h], da_b)
            delta = jnp.sum(prob * d_prob, axis=0, keepdims=True)
            d_score = (prob * (d_prob - delta) * SCALE).astype(BF)
            att[:, part] = dot(vt[...], prob_b).astype(BF)
            back[0, h, part, :] = dot(kt[...], d_score).T.astype(BF)
            dk_acc[...] += dot(d_score, q_b)
            dv_acc[...] += dot(prob_b, da_b)

        back[1, h] = dk_acc[...].astype(BF)
        back[2, h] = dv_acc[...].astype(BF)

        @pl.loop(0, 4)
        def _(c):
            columns = pl.ds(aligned(c, 640), 640)
            grad = dot(att[...], cot[:, columns]).astype(BF)
            for xx in range(4):
                gx[h, xx, :, columns] = grad[xx * 32 : xx * 32 + 16]
                gz[h, c, xx] = grad[xx * 32 + 16 : xx * 32 + 32]

    def first_x(h, p):
        t = ring(x, p + 1)
        return remote(gx.at[h, t], r1x.at[h, p], x1_send.at[h, p], x1_recv.at[h, p], (dp_index(t, z, yh), me))

    def first_z(h, p):
        t = ring(z, p + 1)
        return remote(gz.at[h, t], r1z.at[h, p], z1_send.at[h, p], z1_recv.at[h, p], (dp_index(x, t, yh), me))

    def second_z(h, p):
        t = ring(z, p + 1)
        return remote(s2x.at[h, t], r2x.at[h, p], x2_send.at[h, p], x2_recv.at[h, p], (dp_index(x, t, yh), me))

    def second_x(h, p):
        t = ring(x, p + 1)
        return remote(s2z.at[h, t], r2z.at[h, p], z2_send.at[h, p], z2_recv.at[h, p], (dp_index(t, z, yh), me))

    def third(h):
        return remote(s3.at[h], r3.at[h], y_send.at[h], y_recv.at[h], (dp_index(x, z, 1 - yh), me))

    def after_first(h):
        for p in range(3):
            first_x(h, p).wait_recv()
            first_z(h, p).wait_recv()
        for c in range(4):
            columns = slice(c * 640, (c + 1) * 640)
            total = gx[h, x, :, columns].astype(F32)
            for p in range(3):
                total = total + r1x[h, p, :, columns].astype(F32)
            s2x[h, c] = total.astype(BF)
            total = gz[h, z, c].astype(F32)
            for p in range(3):
                total = total + r1z[h, p, c].astype(F32)
            s2z[h, c] = total.astype(BF)
        for p in range(3):
            second_z(h, p).start()
            second_x(h, p).start()

    def after_second(h):
        for p in range(3):
            second_z(h, p).wait_recv()
            second_x(h, p).wait_recv()
        even = s2x[h, z].astype(F32)
        odd = s2z[h, x].astype(F32)
        for p in range(3):
            even = even + r2x[h, p].astype(F32)
            odd = odd + r2z[h, p].astype(F32)
        first = jnp.full(even.shape, yh, jnp.int32) == 0
        k3[h] = jnp.where(first, even, odd)
        s3[h] = jnp.where(first, odd, even).astype(BF)
        third(h).start()

    @pl.loop(0, HD + 2)
    def _(h):
        @pl.when(h < HD)
        def _():
            for a in range(3):
                head_own(h, a).wait()
                for p in range(3):
                    head_recv(h, a, p).wait_recv()
            compute(h)
            for p in range(3):
                first_x(h, p).start()
                first_z(h, p).start()
            for a in range(3):
                back_own(h, a).start()
                for p in range(3):
                    back_copy(h, a, p).start()

        @pl.when((h >= 1) & (h <= HD))
        def _():
            after_first(h - 1)

        @pl.when(h >= 2)
        def _():
            after_second(h - 2)

    @pl.loop(0, HD)
    def _(h):
        third(h).wait_recv()
        total = (k3[h] + r3[h].astype(F32)).astype(BF)
        for c in range(5):
            rs_out[h * 5 + c] = total[:, c * 128 : (c + 1) * 128]

    for c in range(CC):
        cot_cross(c).wait_send()
        cot_forward(c).wait_send()
    cot_sibling().wait_send()

    @pl.loop(0, HD)
    def _(h):
        for p in range(3):
            first_x(h, p).wait_send()
            first_z(h, p).wait_send()
            second_x(h, p).wait_send()
            second_z(h, p).wait_send()
        third(h).wait_send()
        for a in range(3):
            back_own(h, a).wait()
            for p in range(3):
                head_send(h, a, p).wait_send()
                back_copy(h, a, p).wait_send()
                back_recv_copy(h, a, p).wait_recv()


def attend(q, k, v, cot, w, bias):
    any_space = pl.BlockSpec(memory_space=pl.ANY)
    vmem = pl.BlockSpec(memory_space=pltpu.VMEM)
    sems = lambda *shape: pltpu.SemaphoreType.DMA(shape)
    return pl.pallas_call(
        attend_kernel,
        out_shape=[jax.ShapeDtypeStruct((TOK, OUTW), BF)] * 3 + [jax.ShapeDtypeStruct((25, 16, 128), BF)],
        in_specs=[any_space] * 5 + [vmem],
        out_specs=[any_space] * 3 + [vmem],
        scratch_shapes=[
            pltpu.VMEM((3, HD, LEN, 128), BF),
            pltpu.VMEM((LEN, OUTW), BF),
            pltpu.VMEM((HD * 128, OUTW), BF),
            pltpu.VMEM((HD, LEN, 128), BF),
            pltpu.VMEM((3, HD, LEN, 128), BF),
            pltpu.VMEM((128, LEN), BF),
            pltpu.VMEM((128, LEN), BF),
            pltpu.VMEM((128, LEN), BF),
            pltpu.VMEM((LEN, 128), F32),
            pltpu.VMEM((LEN, 128), F32),
            pltpu.VMEM((HD, 4, 16, OUTW), BF),
            pltpu.VMEM((HD, 4, 4, 16, 640), BF),
            pltpu.VMEM((HD, 3, 16, OUTW), BF),
            pltpu.VMEM((HD, 3, 4, 16, 640), BF),
            pltpu.VMEM((HD, 4, 16, 640), BF),
            pltpu.VMEM((HD, 4, 16, 640), BF),
            pltpu.VMEM((HD, 3, 16, 640), BF),
            pltpu.VMEM((HD, 3, 16, 640), BF),
            pltpu.VMEM((HD, 16, 640), BF),
            pltpu.VMEM((HD, 16, 640), F32),
            pltpu.VMEM((HD, 16, 640), BF),
            sems(2 + 3 * HD),
            sems(HD, 3),
            sems(2 * CC + 1),
            sems(2 * CC + 1),
            *([sems(HD, 3, 3)] * 4),
            *([sems(HD, 3)] * 8),
            sems(HD),
            sems(HD),
        ],
        compiler_params=pltpu.CompilerParams(
            collective_id=0, has_side_effects=True, vmem_limit_bytes=56 * 1024 * 1024
        ),
    )(q, k, v, cot, w, bias)


def adam_step(master_in, first_in, second_in, mean_in, gradient):
    first_out = beta_one * first_in + (1.0 - beta_one) * gradient
    second_out = beta_two * second_in + (1.0 - beta_two) * gradient * gradient
    direction = first_out / bias_one / (jnp.sqrt(second_out / bias_two) + adam_eps)
    master_out = master_in - learn_rate * (direction + weight_decay * master_in)
    mean_out = ema_keep * mean_in + (1.0 - ema_keep) * master_out
    return (master_out, first_out, second_out, mean_out)


def update_kernel(
    rs, slot_from, filled, block_from, master, one, two, mean,
    w_out, master_out, one_out, two_out, mean_out,
    g_all, tx, rx, nb, t_all, nw,
    own_sem, g_send, g_recv, t_send, t_recv, n_send, n_recv, a_send, a_recv, w_send, w_recv,
):
    dp, me, x, z, yh = place_of()
    r = 2 * x + yh

    def member(k):
        j = lax.rem(r + k, 8)
        return j, dp_index(j // 2, z, lax.rem(j, 2))

    def z_peer(p):
        return dp_index(x, ring(z, p + 1), yh)

    barrier = pltpu.get_barrier_semaphore()
    for p in range(3):
        pl.semaphore_signal(barrier, inc=1, device_id=(z_peer(p), me), device_id_type=MESH)
    for k in range(1, 8):
        pl.semaphore_signal(barrier, inc=1, device_id=(member(k)[1], me), device_id_type=MESH)
    pl.semaphore_wait(barrier, 10)

    g_all[z] = rs[...]

    def gather_g(p):
        return remote(rs, g_all.at[z], g_send.at[p], g_recv.at[p], (z_peer(p), me))

    for p in range(3):
        gather_g(p).start()
    for p in range(3):
        gather_g(p).wait_recv()

    def to_owner(k):
        j, device = member(k)
        return remote(tx.at[j], rx.at[r], t_send.at[k - 1], t_recv.at[k - 1], (device, me))

    for k in range(1, 8):
        j, device = member(k)
        for s in range(SL):
            source = slot_from[device * SL + s]
            tx[j, s] = g_all[source // 25, lax.rem(source, 25)]
        to_owner(k).start()
    for s in range(SL):
        source = slot_from[dp * SL + s]
        rx[r, s] = g_all[source // 25, lax.rem(source, 25)]
    for k in range(1, 8):
        to_owner(k).wait_recv()

    for s in range(SL):
        gradient = rx[:, s].astype(F32).reshape(128, 128) * (1.0 / 32.0)
        before = (master[s], one[s], two[s], mean[s])
        stepped = adam_step(*before, gradient)
        keep = jnp.full((128, 128), filled[dp], jnp.int32) > s
        after = [jnp.where(keep, new, old) for new, old in zip(stepped, before)]
        master_out[s], one_out[s], two_out[s], mean_out[s] = after
        nb[:, s] = after[0].astype(BF).reshape(8, 16, 128)

    def from_owner(k):
        j, device = member(k)
        return remote(nb.at[j], t_all.at[z, r], n_send.at[k - 1], n_recv.at[k - 1], (device, me))

    for k in range(1, 8):
        from_owner(k).start()
    t_all[z, r] = nb[r]
    for k in range(1, 8):
        from_owner(k).wait_recv()

    def gather_t(p):
        return remote(t_all.at[z], t_all.at[z], a_send.at[p], a_recv.at[p], (z_peer(p), me))

    for p in range(3):
        gather_t(p).start()
    for p in range(3):
        gather_t(p).wait_recv()

    for h in range(HD):
        for c in range(20):
            source = block_from[h * 20 + c]
            nw[h, :, c * 128 : (c + 1) * 128] = t_all[source // 56, lax.rem(source // 7, 8), lax.rem(source, 7)]

    def gather_w(k):
        return remote(nw, w_out.at[:, r], w_send.at[k - 1], w_recv.at[k - 1], (member(k)[1], me))

    own = pltpu.make_async_copy(nw, w_out.at[:, r], own_sem)
    for k in range(1, 8):
        gather_w(k).start()
    own.start()
    for k in range(1, 8):
        gather_w(k).wait_recv()
    own.wait()
    for p in range(3):
        gather_g(p).wait_send()
        gather_t(p).wait_send()
    for k in range(1, 8):
        to_owner(k).wait_send()
        from_owner(k).wait_send()
        gather_w(k).wait_send()


def update(rs, slot_from, filled, block_from, master, one, two, mean):
    any_space = pl.BlockSpec(memory_space=pl.ANY)
    vmem = pl.BlockSpec(memory_space=pltpu.VMEM)
    smem = pl.BlockSpec(memory_space=pltpu.SMEM)
    sems = lambda *shape: pltpu.SemaphoreType.DMA(shape)
    return pl.pallas_call(
        update_kernel,
        out_shape=[jax.ShapeDtypeStruct((HD, 8, 16, OUTW), BF)] + [jax.ShapeDtypeStruct((SL, 128, 128), F32)] * 4,
        in_specs=[vmem, smem, smem, smem] + [vmem] * 4,
        out_specs=[any_space] + [vmem] * 4,
        scratch_shapes=[
            pltpu.VMEM((4, 25, 16, 128), BF),
            pltpu.VMEM((8, SL, 16, 128), BF),
            pltpu.VMEM((8, SL, 16, 128), BF),
            pltpu.VMEM((8, SL, 16, 128), BF),
            pltpu.VMEM((4, 8, SL, 16, 128), BF),
            pltpu.VMEM((HD, 16, OUTW), BF),
            pltpu.SemaphoreType.DMA,
            sems(3), sems(3), sems(7), sems(7), sems(7), sems(7), sems(3), sems(3), sems(7), sems(7),
        ],
        compiler_params=pltpu.CompilerParams(
            collective_id=1, has_side_effects=True, vmem_limit_bytes=32 * 1024 * 1024
        ),
    )(rs, slot_from, filled, block_from, master, one, two, mean)


def local(q, k, v, cot, w, tile_list, owners, master, one, two, mean):
    listed = jnp.any(tile_list[:, :, None] == jnp.arange(8, dtype=jnp.int32), axis=1)
    bias = jnp.where(listed, 0.0, NEG).astype(F32).reshape(4, 2, 8).transpose(0, 2, 1)
    bias = jnp.broadcast_to(bias[:, :, :, None], (4, 8, 2, 128)).reshape(4, 8, 256)

    group = lax.dynamic_slice_in_dim(owners[:, 0], lax.axis_index("seq") * 100, 100, 0)
    order = jnp.arange(100, dtype=jnp.int32)
    earlier = (group[:, None] == group[None, :]) & (order[None, :] < order[:, None])
    slot_of = jnp.sum(earlier.astype(jnp.int32), axis=1)
    data = jnp.arange(32, dtype=jnp.int32)
    slots = jnp.arange(SL, dtype=jnp.int32)
    filled = jnp.sum((group[None, :] == data[:, None]).astype(jnp.int32), axis=1)
    head, column = order // 20, order % 20
    lies_at = (column // 5) * 25 + head * 5 + column % 5
    match = (group[None, None, :] == data[:, None, None]) & (slot_of[None, None, :] == slots[None, :, None])
    slot_from = jnp.sum(jnp.where(match, lies_at[None, None, :], 0), axis=2).reshape(-1)
    plane = (group // 2) % 4
    block_from = (plane * 8 + (group // 8) * 2 + group % 2) * SL + slot_of

    dq, dk, dv, rs = attend(q, k, v, cot, w, bias)
    new_w, *state = update(rs, slot_from, filled, block_from, master[0], one[0], two[0], mean[0])
    return (dq, dk, dv, new_w.reshape(HD * 128, OUTW), *[s[None] for s in state])


def solution(mesh):
    tokens = P(("dp", "seq"), None)
    state = P("dp", "seq", None, None)
    return jax.shard_map(
        local,
        mesh=mesh,
        in_specs=(tokens,) * 4 + (P("seq", None), P(), P()) + (state,) * 4,
        out_specs=(tokens,) * 3 + (P("seq", None),) + (state,) * 4,
        check_vma=False,
    )
```

```python
import math

import jax
import jax.numpy as jnp
from jax import lax
from jax.experimental import pallas as pl
from jax.experimental.pallas import tpu as pltpu
from jax.sharding import PartitionSpec as P

MESH = pl.DeviceIdType.MESH
BF = jnp.bfloat16
F32 = jnp.float32

learn_rate = 0.001
beta_one = 0.9
beta_two = 0.95
adam_eps = 1e-08
weight_decay = 0.1
ema_keep = 0.99
bias_one = 1.0 - (0.9**50) ** 2
bias_two = 1.0 - (0.95**50) ** 2

HD = 5
TOK = 256
LEN = 1024
OUTW = 2560
SL = 7
NEG = -1e30
SCALE = 1.0 / math.sqrt(128.0)
SCALE2 = SCALE * math.log2(math.e)
CC = 4


def aligned(value, step):
    return pl.multiple_of(value * step, step)


def remote(src, dst, send, recv, device):
    return pltpu.make_async_remote_copy(
        src_ref=src, dst_ref=dst, send_sem=send, recv_sem=recv, device_id=device, device_id_type=MESH
    )


def dot(a, b):
    return lax.dot_general(a, b, (((1,), (0,)), ((), ())), preferred_element_type=F32)


def dot_nt(a, b):
    return lax.dot_general(a, b, (((1,), (1,)), ((), ())), preferred_element_type=F32)


def place_of():
    dp = lax.axis_index("dp")
    return dp, lax.axis_index("seq"), dp // 8, (dp // 2) % 4, dp % 2


def dp_index(x, z, yh):
    return (x * 4 + z) * 2 + yh


def ring(value, step):
    return lax.rem(value + step, 4)


def adam_step(master_in, first_in, second_in, mean_in, gradient):
    first_out = beta_one * first_in + (1.0 - beta_one) * gradient
    second_out = beta_two * second_in + (1.0 - beta_two) * gradient * gradient
    direction = first_out / bias_one / (jnp.sqrt(second_out / bias_two) + adam_eps)
    master_out = master_in - learn_rate * (direction + weight_decay * master_in)
    mean_out = ema_keep * mean_in + (1.0 - ema_keep) * master_out
    return (master_out, first_out, second_out, mean_out)


def step_kernel(
    q_in, k_in, v_in, cot_in, w_in, bias, slot_from, filled, block_from, *refs,
):
    states_in, refs = refs[:4], refs[4:]
    dq_out, dk_out, dv_out, w_out = refs[:4]
    states_out, refs = refs[4:8], refs[8:]
    (
    qkv, cot, w, da, back, kt, vt, att, dk_acc, dv_acc,
    gx, gz, r1x, r1z, s2x, s2z, r2x, r2z, s3, k3, r3,
    local_sem, back_local, cot_send, cot_recv, in_send, in_recv, back_send, back_recv,
    x1_send, x1_recv, z1_send, z1_recv, x2_send, x2_recv, z2_send, z2_recv, y_send, y_recv,
    state, g_all, tx, rx, pieces, landed, w16,
    state_sem, state_out_sem, g_send, g_recv, t_send, t_recv, n_send, n_recv,
    a_send, a_recv, b_send, b_recv,
    ) = refs
    dp, me, x, z, yh = place_of()
    sibling = me + 1 - 2 * lax.rem(me, 2)
    across = ring(me, 2)
    corner = ring(sibling, 2)
    peers = [ring(me, p) for p in (1, 2, 3)]
    sources = [ring(me, 4 - p) for p in (1, 2, 3)]
    inputs = (q_in, k_in, v_in)
    outputs = (dq_out, dk_out, dv_out)

    barrier = pltpu.get_barrier_semaphore()
    for t in peers:
        pl.semaphore_signal(barrier, inc=1, device_id=(dp, t), device_id_type=MESH)
    for k in range(1, 32):
        pl.semaphore_signal(barrier, inc=1, device_id=(lax.rem(dp + k, 32), me), device_id_type=MESH)
    pl.semaphore_wait(barrier, 34)

    def rows(s, n=TOK):
        return pl.ds(aligned(s, TOK), n)

    def cot_rows(s, c):
        return pl.ds(pl.multiple_of(s * TOK + c * (TOK // CC), TOK // CC), TOK // CC)

    def cot_cross(c):
        return remote(
            cot_in.at[pl.ds(c * (TOK // CC), TOK // CC)], cot.at[cot_rows(me, c)],
            cot_send.at[c], cot_recv.at[c], (dp, across),
        )

    def cot_sibling():
        return remote(cot_in, cot.at[rows(me)], cot_send.at[CC], cot_recv.at[CC], (dp, sibling))

    def cot_forward(c):
        part = cot.at[cot_rows(across, c)]
        return remote(part, part, cot_send.at[CC + 1 + c], cot_recv.at[CC + 1 + c], (dp, sibling))

    def cot_own():
        return pltpu.make_async_copy(cot_in, cot.at[rows(me)], local_sem.at[0])

    def w_own():
        return pltpu.make_async_copy(w_in, w, local_sem.at[1])

    def head_columns(t, h):
        return pl.ds(pl.multiple_of((t * HD + h) * 128, 128), 128)

    def head_send(h, a, p):
        t = peers[p]
        return remote(
            inputs[a].at[:, head_columns(t, h)], qkv.at[a, h, rows(me)],
            in_send.at[h, a, p], in_recv.at[h, a, p], (dp, t),
        )

    def head_recv(h, a, p):
        part = qkv.at[a, h, rows(sources[p])]
        return remote(part, part, in_send.at[h, a, p], in_recv.at[h, a, p], (dp, sources[p]))

    def head_own(h, a):
        return pltpu.make_async_copy(
            inputs[a].at[:, head_columns(me, h)], qkv.at[a, h, rows(me)], local_sem.at[2 + 3 * h + a]
        )

    def back_copy(h, a, p):
        t = peers[p]
        return remote(
            back.at[a, h, rows(t)], outputs[a].at[:, head_columns(me, h)],
            back_send.at[h, a, p], back_recv.at[h, a, p], (dp, t),
        )

    def back_recv_copy(h, a, p):
        return remote(
            back.at[a, h, rows(sources[p])], outputs[a].at[:, head_columns(sources[p], h)],
            back_send.at[h, a, p], back_recv.at[h, a, p], (dp, sources[p]),
        )

    def back_own(h, a):
        return pltpu.make_async_copy(
            back.at[a, h, rows(me)], outputs[a].at[:, head_columns(me, h)], back_local.at[h, a]
        )

    def state_copy(i):
        return pltpu.make_async_copy(states_in[i], state.at[i], state_sem.at[i])

    def back_start(h):
        for a in range(3):
            back_own(h, a).start()
            for p in range(3):
                back_copy(h, a, p).start()

    cot_own().start()
    w_own().start()
    for c in range(CC):
        cot_cross(c).start()
    cot_sibling().start()

    @pl.loop(0, HD)
    def _(h):
        for a in range(3):
            head_own(h, a).start()
            for p in range(3):
                head_send(h, a, p).start()

    for i in range(4):
        state_copy(i).start()
    for c in range(CC):
        cot_cross(c).wait_recv()
        cot_forward(c).start()
    cot_own().wait()
    w_own().wait()
    cot_sibling().wait_recv()
    for c in range(CC):
        cot_forward(c).wait_recv()

    @pl.loop(0, 4)
    def _(b):
        d_rows = dot_nt(cot[pl.ds(aligned(b, 256), 256), :], w[...]).astype(BF)
        for h in range(HD):
            da[h, pl.ds(aligned(b, 256), 256), :] = d_rows[:, h * 128 : (h + 1) * 128]

    def compute(h):
        kt[...] = qkv[1, h].T
        vt[...] = qkv[2, h].T
        dk_acc[...] = jnp.zeros_like(dk_acc)
        dv_acc[...] = jnp.zeros_like(dv_acc)

        @pl.loop(0, 4)
        def _(b):
            part = pl.ds(aligned(b, 256), 256)
            q_b = qkv[0, h, part, :]
            da_b = da[h, part, :]
            score = dot_nt(qkv[1, h], q_b).reshape(8, 128, 256) * SCALE2 + bias[b][:, None, :]
            score = score.reshape(LEN, 256)
            top = jnp.max(score, axis=0, keepdims=True)
            weight = jnp.exp2(score - top)
            total = jnp.sum(weight, axis=0, keepdims=True)
            prob = weight * (1.0 / total)
            prob_b = prob.astype(BF)
            d_prob = dot_nt(qkv[2, h], da_b)
            delta = jnp.sum(prob * d_prob, axis=0, keepdims=True)
            d_score = (prob * (d_prob - delta) * SCALE).astype(BF)
            att[:, part] = dot(vt[...], prob_b).astype(BF)
            back[0, h, part, :] = dot(kt[...], d_score).T.astype(BF)
            dk_acc[...] += dot(d_score, q_b)
            dv_acc[...] += dot(prob_b, da_b)

        back[1, h] = dk_acc[...].astype(BF)
        back[2, h] = dv_acc[...].astype(BF)

        @pl.loop(0, 4)
        def _(c):
            columns = pl.ds(aligned(c, 640), 640)
            grad = dot(att[...], cot[:, columns]).astype(BF)
            for xx in range(4):
                gx[h, xx, :, columns] = grad[xx * 32 : xx * 32 + 16]
                gz[h, c, xx] = grad[xx * 32 + 16 : xx * 32 + 32]

    def first_x(h, p):
        t = ring(x, p + 1)
        return remote(gx.at[h, t], r1x.at[h, p], x1_send.at[h, p], x1_recv.at[h, p], (dp_index(t, z, yh), me))

    def first_z(h, p):
        t = ring(z, p + 1)
        return remote(gz.at[h, t], r1z.at[h, p], z1_send.at[h, p], z1_recv.at[h, p], (dp_index(x, t, yh), me))

    def second_z(h, p):
        t = ring(z, p + 1)
        return remote(s2x.at[h, t], r2x.at[h, p], x2_send.at[h, p], x2_recv.at[h, p], (dp_index(x, t, yh), me))

    def second_x(h, p):
        t = ring(x, p + 1)
        return remote(s2z.at[h, t], r2z.at[h, p], z2_send.at[h, p], z2_recv.at[h, p], (dp_index(t, z, yh), me))

    def third(h):
        return remote(s3.at[h], r3.at[h], y_send.at[h], y_recv.at[h], (dp_index(x, z, 1 - yh), me))

    def after_first(h):
        for p in range(3):
            first_x(h, p).wait_recv()
            first_z(h, p).wait_recv()
        for c in range(4):
            columns = slice(c * 640, (c + 1) * 640)
            total = gx[h, x, :, columns].astype(F32)
            for p in range(3):
                total = total + r1x[h, p, :, columns].astype(F32)
            s2x[h, c] = total.astype(BF)
            total = gz[h, z, c].astype(F32)
            for p in range(3):
                total = total + r1z[h, p, c].astype(F32)
            s2z[h, c] = total.astype(BF)
        for p in range(3):
            second_z(h, p).start()
            second_x(h, p).start()

    def after_second(h):
        for p in range(3):
            second_z(h, p).wait_recv()
            second_x(h, p).wait_recv()
        even = s2x[h, z].astype(F32)
        odd = s2z[h, x].astype(F32)
        for p in range(3):
            even = even + r2x[h, p].astype(F32)
            odd = odd + r2z[h, p].astype(F32)
        first = jnp.full(even.shape, yh, jnp.int32) == 0
        k3[h] = jnp.where(first, even, odd)
        s3[h] = jnp.where(first, odd, even).astype(BF)
        third(h).start()

    @pl.loop(0, HD + 2)
    def _(h):
        @pl.when(h < HD)
        def _():
            for a in range(3):
                head_own(h, a).wait()
                for p in range(3):
                    head_recv(h, a, p).wait_recv()

            @pl.when(h == HD - 1)
            def _():
                @pl.loop(0, HD - 1)
                def _(g):
                    back_start(g)

            compute(h)
            for p in range(3):
                first_x(h, p).start()
                first_z(h, p).start()
            @pl.when(h == HD - 1)
            def _():
                back_start(HD - 1)

        @pl.when((h >= 1) & (h <= HD))
        def _():
            after_first(h - 1)

        @pl.when(h >= 2)
        def _():
            after_second(h - 2)

    @pl.loop(0, HD)
    def _(h):
        third(h).wait_recv()
        total = (k3[h] + r3[h].astype(F32)).astype(BF)
        for c in range(5):
            g_all[z, h * 5 + c] = total[:, c * 128 : (c + 1) * 128]

    r = 2 * x + yh

    def member(k):
        j = lax.rem(r + k, 8)
        return j, dp_index(j // 2, z, lax.rem(j, 2))

    def gather_g(p):
        device = dp_index(x, ring(z, p + 1), yh)
        return remote(g_all.at[z], g_all.at[z], g_send.at[p], g_recv.at[p], (device, me))

    for p in range(3):
        gather_g(p).start()
    for p in range(3):
        gather_g(p).wait_recv()

    def to_owner(k):
        j, device = member(k)
        return remote(tx.at[j], rx.at[r], t_send.at[k - 1], t_recv.at[k - 1], (device, me))

    for k in range(1, 8):
        j, device = member(k)
        for s in range(SL):
            source = slot_from[device * SL + s]
            tx[j, s] = g_all[source // 25, lax.rem(source, 25)]
        to_owner(k).start()
    for s in range(SL):
        source = slot_from[dp * SL + s]
        rx[r, s] = g_all[source // 25, lax.rem(source, 25)]
    for i in range(4):
        state_copy(i).wait()
    for k in range(1, 8):
        to_owner(k).wait_recv()

    def state_out(i):
        return pltpu.make_async_copy(state.at[i], states_out[i], state_out_sem.at[i])

    even = None
    for s in range(SL):
        gradient = rx[:, s].astype(F32).reshape(128, 128) * (1.0 / 32.0)
        before = [state[i, s] for i in range(4)]
        stepped = adam_step(*before, gradient)
        keep = jnp.full((128, 128), filled[dp], jnp.int32) > s
        after = [jnp.where(keep, new, old) for new, old in zip(stepped, before)]
        for i in range(4):
            state[i, s] = after[i]
        fresh = after[0].reshape(16, 8, 128)
        if s % 2 == 0:
            even = fresh
        if s % 2 == 1 or s == SL - 1:
            pieces[:, s // 2] = jnp.concatenate([even, fresh], axis=1).astype(BF)
    mine = 4 * x + z

    def from_owner(k):
        device = lax.rem(dp + k, 32)
        return remote(pieces.at[device // 2], landed.at[dp], n_send.at[k - 1], n_recv.at[k - 1], (device, me))

    for k in range(1, 32):
        from_owner(k).start()
    for i in range(4):
        state_out(i).start()
    landed[dp] = pieces[mine]
    for k in range(1, 32):
        from_owner(k).wait_recv()

    for pair in range(50):
        halves = []
        for b in (2 * pair, 2 * pair + 1):
            source = block_from[b]
            tile = landed[source // 8, lax.rem(source, 8) // 2].astype(F32)
            odd = jnp.full((8, 128), lax.rem(source, 2), jnp.int32) == 1
            halves.append(jnp.where(odd, tile[8:], tile[:8]))
        w16[x, z, pair] = jnp.concatenate(halves, axis=0).astype(BF)

    near, far = pl.ds(0, 25), pl.ds(25, 25)

    def gather_x(p, i, part, send, recv):
        place = w16.at[x, ring(z, i), part]
        return remote(place, place, send.at[p, i], recv.at[p, i], (dp_index(ring(x, p + 1), z, yh), me))

    def gather_z(p, i, part, send, recv):
        place = w16.at[ring(x, i), z, part]
        return remote(place, place, send.at[p, i], recv.at[p, i], (dp_index(x, ring(z, p + 1), yh), me))

    def landed_x(p, i, part, send, recv):
        place = w16.at[ring(x, 3 - p), ring(z, i), part]
        return remote(place, place, send.at[p, i], recv.at[p, i], (dp_index(ring(x, 3 - p), z, yh), me))

    def landed_z(p, i, part, send, recv):
        place = w16.at[ring(x, i), ring(z, 3 - p), part]
        return remote(place, place, send.at[p, i], recv.at[p, i], (dp_index(x, ring(z, 3 - p), yh), me))

    ax, az = (a_send.at[0], a_recv.at[0]), (a_send.at[1], a_recv.at[1])
    bx, bz = (b_send.at[0], b_recv.at[0]), (b_send.at[1], b_recv.at[1])
    for p in range(3):
        gather_x(p, 0, near, *ax).start()
        gather_z(p, 0, far, *bz).start()
    for p in range(3):
        gather_z(p, 0, near, *az).start()
        gather_x(p, 0, far, *bx).start()
    for i in range(3):
        landed_x(i, 0, near, *ax).wait_recv()
        landed_z(i, 0, far, *bz).wait_recv()
        for p in range(3):
            gather_z(p, 3 - i, near, *az).start()
            gather_x(p, 3 - i, far, *bx).start()
    for p in range(3):
        for i in range(4):
            landed_z(p, i, near, *az).wait_recv()
            landed_x(p, i, far, *bx).wait_recv()

    @pl.loop(0, HD)
    def _(h):
        for c in range(10):
            for j in range(8):
                low = w16[j // 2, 2 * (j % 2), h * 10 + c].astype(F32)
                high = w16[j // 2, 2 * (j % 2) + 1, h * 10 + c].astype(F32)
                left = jnp.concatenate([low[:8], high[:8]], axis=0)
                right = jnp.concatenate([low[8:], high[8:]], axis=0)
                w_out[h, j * 16 : (j + 1) * 16, c * 256 : c * 256 + 128] = left.astype(BF)
                w_out[h, j * 16 : (j + 1) * 16, c * 256 + 128 : c * 256 + 256] = right.astype(BF)

    for c in range(CC):
        cot_cross(c).wait_send()
        cot_forward(c).wait_send()
    cot_sibling().wait_send()

    @pl.loop(0, HD)
    def _(h):
        for p in range(3):
            first_x(h, p).wait_send()
            first_z(h, p).wait_send()
            second_x(h, p).wait_send()
            second_z(h, p).wait_send()
        third(h).wait_send()
        for a in range(3):
            back_own(h, a).wait()
            for p in range(3):
                head_send(h, a, p).wait_send()
                back_copy(h, a, p).wait_send()
                back_recv_copy(h, a, p).wait_recv()

    for p in range(3):
        gather_g(p).wait_send()
        gather_x(p, 0, near, *ax).wait_send()
        gather_z(p, 0, far, *bz).wait_send()
        for i in range(4):
            gather_z(p, i, near, *az).wait_send()
            gather_x(p, i, far, *bx).wait_send()
    for k in range(1, 8):
        to_owner(k).wait_send()
    for k in range(1, 32):
        from_owner(k).wait_send()
    for i in range(4):
        state_out(i).wait()


def step(q, k, v, cot, w, bias, slot_from, filled, block_from, *states):
    any_space = pl.BlockSpec(memory_space=pl.ANY)
    vmem = pl.BlockSpec(memory_space=pltpu.VMEM)
    smem = pl.BlockSpec(memory_space=pltpu.SMEM)
    sems = lambda *shape: pltpu.SemaphoreType.DMA(shape)
    return pl.pallas_call(
        step_kernel,
        out_shape=[jax.ShapeDtypeStruct((TOK, OUTW), BF)] * 3 + [jax.ShapeDtypeStruct((HD, 128, OUTW), BF)]
        + [jax.ShapeDtypeStruct((SL, 128, 128), F32)] * 4,
        in_specs=[any_space] * 5 + [vmem] + [smem] * 3 + [any_space] * 4,
        out_specs=[any_space] * 3 + [vmem] + [any_space] * 4,
        scratch_shapes=[
            pltpu.VMEM((3, HD, LEN, 128), BF),
            pltpu.VMEM((LEN, OUTW), BF),
            pltpu.VMEM((HD * 128, OUTW), BF),
            pltpu.VMEM((HD, LEN, 128), BF),
            pltpu.VMEM((3, HD, LEN, 128), BF),
            pltpu.VMEM((128, LEN), BF),
            pltpu.VMEM((128, LEN), BF),
            pltpu.VMEM((128, LEN), BF),
            pltpu.VMEM((LEN, 128), F32),
            pltpu.VMEM((LEN, 128), F32),
            pltpu.VMEM((HD, 4, 16, OUTW), BF),
            pltpu.VMEM((HD, 4, 4, 16, 640), BF),
            pltpu.VMEM((HD, 3, 16, OUTW), BF),
            pltpu.VMEM((HD, 3, 4, 16, 640), BF),
            pltpu.VMEM((HD, 4, 16, 640), BF),
            pltpu.VMEM((HD, 4, 16, 640), BF),
            pltpu.VMEM((HD, 3, 16, 640), BF),
            pltpu.VMEM((HD, 3, 16, 640), BF),
            pltpu.VMEM((HD, 16, 640), BF),
            pltpu.VMEM((HD, 16, 640), F32),
            pltpu.VMEM((HD, 16, 640), BF),
            sems(2 + 3 * HD),
            sems(HD, 3),
            sems(2 * CC + 1),
            sems(2 * CC + 1),
            *([sems(HD, 3, 3)] * 4),
            *([sems(HD, 3)] * 8),
            sems(HD),
            sems(HD),
            pltpu.VMEM((4, SL, 128, 128), F32),
            pltpu.VMEM((4, 25, 16, 128), BF),
            pltpu.VMEM((8, SL, 16, 128), BF),
            pltpu.VMEM((8, SL, 16, 128), BF),
            pltpu.VMEM((16, 4, 16, 128), BF),
            pltpu.VMEM((32, 4, 16, 128), BF),
            pltpu.VMEM((4, 4, 50, 16, 128), BF),
            sems(4),
            sems(4),
            sems(3),
            sems(3),
            sems(7),
            sems(7),
            sems(31),
            sems(31),
            sems(2, 3, 4),
            sems(2, 3, 4),
            sems(2, 3, 4),
            sems(2, 3, 4),
        ],
        compiler_params=pltpu.CompilerParams(
            collective_id=0, has_side_effects=True, vmem_limit_bytes=56 * 1024 * 1024
        ),
    )(q, k, v, cot, w, bias, slot_from, filled, block_from, *states)


def local(q, k, v, cot, w, tile_list, owners, master, one, two, mean):
    listed = jnp.any(tile_list[:, :, None] == jnp.arange(8, dtype=jnp.int32), axis=1)
    bias = jnp.where(listed, 0.0, NEG).astype(F32).reshape(4, 2, 8).transpose(0, 2, 1)
    bias = jnp.broadcast_to(bias[:, :, :, None], (4, 8, 2, 128)).reshape(4, 8, 256)

    group = lax.dynamic_slice_in_dim(owners[:, 0], lax.axis_index("seq") * 100, 100, 0)
    order = jnp.arange(100, dtype=jnp.int32)
    earlier = (group[:, None] == group[None, :]) & (order[None, :] < order[:, None])
    slot_of = jnp.sum(earlier.astype(jnp.int32), axis=1)
    data = jnp.arange(32, dtype=jnp.int32)
    slots = jnp.arange(SL, dtype=jnp.int32)
    filled = jnp.sum((group[None, :] == data[:, None]).astype(jnp.int32), axis=1)
    head, column = order // 20, order % 20
    lies_at = (column // 5) * 25 + head * 5 + column % 5
    match = (group[None, None, :] == data[:, None, None]) & (slot_of[None, None, :] == slots[None, :, None])
    slot_from = jnp.sum(jnp.where(match, lies_at[None, None, :], 0), axis=2).reshape(-1)
    block_from = group * 8 + slot_of

    dq, dk, dv, new_w, *states = step(
        q, k, v, cot, w, bias, slot_from, filled, block_from, master[0], one[0], two[0], mean[0]
    )
    return (dq, dk, dv, new_w.reshape(HD * 128, OUTW), *[s[None] for s in states])


def solution(mesh):
    tokens = P(("dp", "seq"), None)
    state = P("dp", "seq", None, None)
    return jax.shard_map(
        local,
        mesh=mesh,
        in_specs=(tokens,) * 4 + (P("seq", None), P(), P()) + (state,) * 4,
        out_specs=(tokens,) * 3 + (P("seq", None),) + (state,) * 4,
        check_vma=False,
    )
```

```python
import math

import jax
import jax.numpy as jnp
from jax import lax
from jax.experimental import pallas as pl
from jax.experimental.pallas import tpu as pltpu
from jax.sharding import PartitionSpec as P

MESH = pl.DeviceIdType.MESH
BF = jnp.bfloat16
F32 = jnp.float32

learn_rate = 0.001
beta_one = 0.9
beta_two = 0.95
adam_eps = 1e-08
weight_decay = 0.1
ema_keep = 0.99
bias_one = 1.0 - (0.9**50) ** 2
bias_two = 1.0 - (0.95**50) ** 2

HD = 5
TOK = 256
LEN = 1024
OUTW = 2560
SL = 7
NEG = -1e30
SCALE = 1.0 / math.sqrt(128.0)
SCALE2 = SCALE * math.log2(math.e)
BACK_ONE, BACK_TWO = 6, 8
CC = 4


def aligned(value, step):
    return pl.multiple_of(value * step, step)


def remote(src, dst, send, recv, device):
    return pltpu.make_async_remote_copy(
        src_ref=src, dst_ref=dst, send_sem=send, recv_sem=recv, device_id=device, device_id_type=MESH
    )


def dot(a, b):
    return lax.dot_general(a, b, (((1,), (0,)), ((), ())), preferred_element_type=F32)


def dot_nt(a, b):
    return lax.dot_general(a, b, (((1,), (1,)), ((), ())), preferred_element_type=F32)


def place_of():
    dp = lax.axis_index("dp")
    return dp, lax.axis_index("seq"), dp // 8, (dp // 2) % 4, dp % 2


def dp_index(x, z, yh):
    return (x * 4 + z) * 2 + yh


def ring(value, step):
    return lax.rem(value + step, 4)


def adam_step(master_in, first_in, second_in, mean_in, gradient):
    first_out = beta_one * first_in + (1.0 - beta_one) * gradient
    second_out = beta_two * second_in + (1.0 - beta_two) * gradient * gradient
    direction = first_out / bias_one / (jnp.sqrt(second_out / bias_two) + adam_eps)
    master_out = master_in - learn_rate * (direction + weight_decay * master_in)
    mean_out = ema_keep * mean_in + (1.0 - ema_keep) * master_out
    return (master_out, first_out, second_out, mean_out)


def step_kernel(
    q_in, k_in, v_in, cot_in, w_in, tile_list, owners, *refs,
):
    states_in, refs = refs[:4], refs[4:]
    dq_out, dk_out, dv_out, w_out = refs[:4]
    states_out, refs = refs[4:8], refs[8:]
    (
    qkv, cot, w, da, back, kt, vt, att, probs, dk_acc, dv_acc,
    gx, gz, r1x, r1z, s2x, s2z, r2x, r2z, sums,
    local_sem, back_local, cot_send, cot_recv, in_send, in_recv, back_send, back_recv,
    x1_send, x1_recv, z1_send, z1_recv, x2_send, x2_recv, z2_send, z2_recv,
    state, tx, rx, pieces, landed, w16,
    state_sem, state_out_sem, t_send, t_recv, n_send, n_recv,
    a_send, a_recv, b_send, b_recv,
    bias, slot_table, block_table, slot_from, block_from, table_sem,
    ) = refs
    dp, me, x, z, yh = place_of()
    sibling = me + 1 - 2 * lax.rem(me, 2)
    across = ring(me, 2)
    corner = ring(sibling, 2)
    peers = [ring(me, p) for p in (1, 2, 3)]
    sources = [ring(me, 4 - p) for p in (1, 2, 3)]
    inputs = (q_in, k_in, v_in)
    outputs = (dq_out, dk_out, dv_out)

    barrier = pltpu.get_barrier_semaphore()
    for t in peers:
        pl.semaphore_signal(barrier, inc=1, device_id=(dp, t), device_id_type=MESH)
    for k in range(1, 32):
        pl.semaphore_signal(barrier, inc=1, device_id=(lax.rem(dp + k, 32), me), device_id_type=MESH)
    pl.semaphore_wait(barrier, 34)

    def rows(s, n=TOK):
        return pl.ds(aligned(s, TOK), n)

    def cot_rows(s, c):
        return pl.ds(pl.multiple_of(s * TOK + c * (TOK // CC), TOK // CC), TOK // CC)

    def cot_cross(c):
        return remote(
            cot_in.at[pl.ds(c * (TOK // CC), TOK // CC)], cot.at[cot_rows(me, c)],
            cot_send.at[c], cot_recv.at[c], (dp, across),
        )

    def cot_sibling():
        return remote(cot_in, cot.at[rows(me)], cot_send.at[CC], cot_recv.at[CC], (dp, sibling))

    def cot_forward(c):
        part = cot.at[cot_rows(across, c)]
        return remote(part, part, cot_send.at[CC + 1 + c], cot_recv.at[CC + 1 + c], (dp, sibling))

    def cot_own():
        return pltpu.make_async_copy(cot_in, cot.at[rows(me)], local_sem.at[0])

    def w_own():
        return pltpu.make_async_copy(w_in, w, local_sem.at[1])

    def head_columns(t, h):
        return pl.ds(pl.multiple_of((t * HD + h) * 128, 128), 128)

    def head_send(h, a, p):
        t = peers[p]
        return remote(
            inputs[a].at[:, head_columns(t, h)], qkv.at[a, h, rows(me)],
            in_send.at[h, a, p], in_recv.at[h, a, p], (dp, t),
        )

    def head_recv(h, a, p):
        part = qkv.at[a, h, rows(sources[p])]
        return remote(part, part, in_send.at[h, a, p], in_recv.at[h, a, p], (dp, sources[p]))

    def head_own(h, a):
        return pltpu.make_async_copy(
            inputs[a].at[:, head_columns(me, h)], qkv.at[a, h, rows(me)], local_sem.at[2 + 3 * h + a]
        )

    def back_copy(h, a, p):
        t = peers[p]
        return remote(
            back.at[a, h, rows(t)], outputs[a].at[:, head_columns(me, h)],
            back_send.at[h, a, p], back_recv.at[h, a, p], (dp, t),
        )

    def back_recv_copy(h, a, p):
        return remote(
            back.at[a, h, rows(sources[p])], outputs[a].at[:, head_columns(sources[p], h)],
            back_send.at[h, a, p], back_recv.at[h, a, p], (dp, sources[p]),
        )

    def back_own(h, a):
        return pltpu.make_async_copy(
            back.at[a, h, rows(me)], outputs[a].at[:, head_columns(me, h)], back_local.at[h, a]
        )

    def state_copy(i):
        return pltpu.make_async_copy(states_in[i], state.at[i], state_sem.at[i])

    def back_start(first, last):
        @pl.loop(first, last)
        def _(unit):
            h, a = unit // 3, lax.rem(unit, 3)
            for i in range(3):

                @pl.when(a == i)
                def _():
                    back_own(h, i).start()
                    for p in range(3):
                        back_copy(h, i, p).start()

    cot_own().start()
    w_own().start()
    for c in range(CC):
        cot_cross(c).start()
    cot_sibling().start()

    @pl.loop(0, HD)
    def _(h):
        for a in range(3):
            head_own(h, a).start()
            for p in range(3):
                head_send(h, a, p).start()

    for i in range(4):
        state_copy(i).start()

    for i in range(8):
        for n in range(8):
            listed = tile_list[i, 0] == n
            for j in range(1, 6):
                listed = listed | (tile_list[i, j] == n)
            low = jnp.where(listed, 0.0, NEG).astype(F32)
            bias[i // 2, n : n + 1, (i % 2) * 128 : (i % 2) * 128 + 128] = jnp.full((1, 128), low, F32)

    lane = lax.broadcasted_iota(jnp.int32, (128, 128), 1)
    row = lax.broadcasted_iota(jnp.int32, (128, 128), 0)

    def put(b, held):
        return jnp.where(lane[:8] == b, owners[me * 100 + b], held)

    owner = lax.fori_loop(0, 100, put, jnp.full((8, 128), -1, jnp.int32))
    owner = jnp.broadcast_to(owner[:1], (128, 128))
    earlier = (owner.T == owner) & (row < lane)
    slot_of = jnp.sum(jnp.where(earlier, 1, 0), axis=0, keepdims=True)
    block_table[...] = jnp.broadcast_to(owner[:1] * 8 + slot_of, (8, 128))
    owned = owner[:32] == row[:32]
    for s in range(SL):
        match = owned & (jnp.broadcast_to(slot_of, (32, 128)) == s)
        block = jnp.sum(jnp.where(match, lane[:32], 0), axis=1, keepdims=True)
        slot_table[s] = jnp.broadcast_to(block, (32, 128))
    count = jnp.sum(jnp.where(owned, 1, 0), axis=1, keepdims=True)
    slot_table[SL] = jnp.broadcast_to(count, (32, 128))
    tables = (
        pltpu.make_async_copy(slot_table, slot_from, table_sem.at[0]),
        pltpu.make_async_copy(block_table, block_from, table_sem.at[1]),
    )
    for table in tables:
        table.start()
    for table in tables:
        table.wait()

    for c in range(CC):
        cot_cross(c).wait_recv()
        cot_forward(c).start()
    cot_own().wait()
    w_own().wait()
    cot_sibling().wait_recv()
    for c in range(CC):
        cot_forward(c).wait_recv()

    @pl.loop(0, 4)
    def _(b):
        d_rows = dot_nt(cot[pl.ds(aligned(b, 256), 256), :], w[...]).astype(BF)
        for h in range(HD):
            da[h, pl.ds(aligned(b, 256), 256), :] = d_rows[:, h * 128 : (h + 1) * 128]

    def forward(h):
        vt[...] = qkv[2, h].T
        for b in range(4):
            part = slice(b * 256, b * 256 + 256)
            score = dot_nt(qkv[1, h], qkv[0, h, part, :]).reshape(8, 128, 256) * SCALE2 + bias[b][:, None, :]
            score = score.reshape(LEN, 256)
            top = jnp.max(score, axis=0, keepdims=True)
            weight = jnp.exp2(score - top)
            total = jnp.sum(weight, axis=0, keepdims=True)
            prob = weight * (1.0 / total)
            probs[lax.rem(h, 2), b] = prob
            att[:, part] = dot(vt[...], prob.astype(BF)).astype(BF)

        @pl.loop(0, 2)
        def _(c):
            columns = pl.ds(aligned(c, 640), 640)
            grad = dot(att[...], cot[:, columns]).astype(BF)
            for xx in range(4):
                gx[h, xx, :, columns] = grad[xx * 32 : xx * 32 + 32]
            grad = dot(att[...], cot[:, pl.ds(pl.multiple_of(1280 + c * 640, 640), 640)])
            for zz in range(4):
                rows_z = [grad[a * 32 + zz * 8 : a * 32 + zz * 8 + 8] for a in range(4)]
                gz[h, zz, :, columns] = jnp.concatenate(rows_z, axis=0).astype(BF)

    def backward(h):
        kt[...] = qkv[1, h].T
        dk_acc[...] = jnp.zeros_like(dk_acc)
        dv_acc[...] = jnp.zeros_like(dv_acc)
        for b in range(4):
            part = slice(b * 256, b * 256 + 256)
            q_b = qkv[0, h, part, :]
            da_b = da[h, part, :]
            prob = probs[lax.rem(h, 2), b]
            d_prob = dot_nt(qkv[2, h], da_b)
            delta = jnp.sum(prob * d_prob, axis=0, keepdims=True)
            d_score = (prob * (d_prob - delta) * SCALE).astype(BF)
            back[0, h, part, :] = dot(kt[...], d_score).T.astype(BF)
            dk_acc[...] += dot(d_score, q_b)
            dv_acc[...] += dot(prob.astype(BF), da_b)

        back[1, h] = dk_acc[...].astype(BF)
        back[2, h] = dv_acc[...].astype(BF)

    def first_x(h, p):
        t = ring(x, p + 1)
        return remote(gx.at[h, t], r1x.at[h, p], x1_send.at[h, p], x1_recv.at[h, p], (dp_index(t, z, yh), me))

    def first_z(h, p):
        t = ring(z, p + 1)
        return remote(gz.at[h, t], r1z.at[h, p], z1_send.at[h, p], z1_recv.at[h, p], (dp_index(x, t, yh), me))

    def second_z(h, p):
        t = ring(z, p + 1)
        return remote(s2x.at[h, t], r2x.at[h, p], x2_send.at[h, p], x2_recv.at[h, p], (dp_index(x, t, yh), me))

    def second_x(h, p):
        t = ring(x, p + 1)
        return remote(s2z.at[h, t], r2z.at[h, p], z2_send.at[h, p], z2_recv.at[h, p], (dp_index(t, z, yh), me))

    def after_first(h):
        for p in range(3):
            first_x(h, p).wait_recv()
            first_z(h, p).wait_recv()
        total = gx[h, x].astype(F32)
        for p in range(3):
            total = total + r1x[h, p].astype(F32)
        for t in range(4):
            part = total[t * 8 : t * 8 + 8]
            s2x[h, t] = jnp.concatenate([part[:, :640], part[:, 640:]], axis=0).astype(BF)
        total = gz[h, z].astype(F32)
        for p in range(3):
            total = total + r1z[h, p].astype(F32)
        for t in range(4):
            part = total[t * 8 : t * 8 + 8]
            s2z[h, t] = jnp.concatenate([part[:, :640], part[:, 640:]], axis=0).astype(BF)
        for p in range(3):
            second_z(h, p).start()
            second_x(h, p).start()

    def after_second(h):
        for p in range(3):
            second_z(h, p).wait_recv()
            second_x(h, p).wait_recv()
        even = s2x[h, z].astype(F32)
        odd = s2z[h, x].astype(F32)
        for p in range(3):
            even = even + r2x[h, p].astype(F32)
            odd = odd + r2z[h, p].astype(F32)
        for i, total in enumerate((even, odd)):
            for u in range(2):
                for c in range(5):
                    sums[h * 20 + i * 10 + u * 5 + c] = total[u * 8 : u * 8 + 8, c * 128 : c * 128 + 128]

    @pl.loop(0, HD)
    def _(h):
        for a in range(3):
            head_own(h, a).wait()
            for p in range(3):
                head_recv(h, a, p).wait_recv()

        @pl.when(h == HD - 1)
        def _():
            back_start(0, BACK_ONE)

        forward(h)
        for p in range(3):
            first_x(h, p).start()
            first_z(h, p).start()

        @pl.when(h >= 1)
        def _():
            after_first(h - 1)
            backward(h - 1)
            after_second(h - 1)

    after_first(HD - 1)
    after_second(HD - 1)

    def pack(device):
        tiles = [sums[jnp.clip(slot_from[s, device, 0], 0, HD * 20 - 1)] for s in range(SL)]
        for t in range(4):
            tx[device, t] = jnp.concatenate([tiles[2 * t], tiles[min(2 * t + 1, SL - 1)]], axis=0).astype(BF)

    def to_owner(k):
        device = lax.rem(dp + k, 32)
        return remote(tx.at[device], rx.at[dp], t_send.at[k - 1], t_recv.at[k - 1], (device, me))

    @pl.loop(1, 32)
    def _(k):
        pack(lax.rem(dp + k, 32))
        to_owner(k).start()

    back_start(BACK_ONE, BACK_TWO)
    backward(HD - 1)
    pack(dp)
    rx[dp] = tx[dp]
    for i in range(4):
        state_copy(i).wait()

    @pl.loop(1, 32)
    def _(k):
        to_owner(k).wait_recv()

    def state_out(i):
        return pltpu.make_async_copy(state.at[i], states_out[i], state_out_sem.at[i])

    arrived = rx[...].reshape(16, 2, 4, 16, 128)
    even = None
    for s in range(SL):
        if s % 2 == 0:
            both = arrived[:, 0, s // 2].astype(F32) + arrived[:, 1, s // 2].astype(F32)
        half = both[:, :8] if s % 2 == 0 else both[:, 8:]
        gradient = half.reshape(128, 128) * (1.0 / 32.0)
        before = [state[i, s] for i in range(4)]
        stepped = adam_step(*before, gradient)
        keep = jnp.full((128, 128), slot_from[SL, dp, 0], jnp.int32) > s
        after = [jnp.where(keep, new, old) for new, old in zip(stepped, before)]
        for i in range(4):
            state[i, s] = after[i]
        fresh = after[0].reshape(16, 8, 128)
        if s % 2 == 0:
            even = fresh
        if s % 2 == 1 or s == SL - 1:
            pieces[:, s // 2] = jnp.concatenate([even, fresh], axis=1).astype(BF)
    mine = 4 * x + z

    def from_owner(k):
        device = lax.rem(dp + k, 32)
        return remote(pieces.at[device // 2], landed.at[dp], n_send.at[k - 1], n_recv.at[k - 1], (device, me))

    @pl.loop(1, 32)
    def _(k):
        from_owner(k).start()

    back_start(BACK_TWO, 3 * HD)
    for i in range(4):
        state_out(i).start()
    landed[dp] = pieces[mine]

    @pl.loop(1, 32)
    def _(k):
        from_owner(k).wait_recv()

    def arrange(pairs):
        for pair in pairs:
            halves = []
            for b in (2 * pair, 2 * pair + 1):
                source = jnp.clip(block_from[0, b], 0, 255)
                tile = landed[source // 8, lax.rem(source, 8) // 2].astype(F32)
                odd = jnp.full((8, 128), lax.rem(source, 2), jnp.int32) == 1
                halves.append(jnp.where(odd, tile[8:], tile[:8]))
            w16[x, z, pair] = jnp.concatenate(halves, axis=0).astype(BF)

    here = ((x, z), (z, x))

    def device_of(f, first, second):
        a, b = (first, second) if f == 0 else (second, first)
        return (dp_index(a, b, yh), me)

    def piece(f, first, second, d, kind):
        start, size = f * 25, 25
        if kind == 1:
            start, size = (start, 12) if d == 0 else (start + 12, 13)
        a, b = (first, second) if f == 0 else (second, first)
        return w16.at[a, b, pl.ds(start, size)]

    ways = (1, 3)

    def ring_one(f, d, kind):
        a, b = here[f]
        place = piece(f, a if kind == 0 else ring(a, ways[1 - d]), b, d, kind)
        return remote(place, place, a_send.at[f, d, kind], a_recv.at[f, d, kind], device_of(f, ring(a, ways[d]), b))

    def landed_one(f, d, kind):
        a, b = here[f]
        place = piece(f, ring(a, ways[1 - d]) if kind == 0 else ring(a, 2), b, d, kind)
        return remote(place, place, a_send.at[f, d, kind], a_recv.at[f, d, kind], device_of(f, ring(a, ways[1 - d]), b))

    def ring_two(f, i, d, kind):
        a, b = here[f]
        place = piece(f, ring(a, i), b if kind == 0 else ring(b, ways[1 - d]), d, kind)
        to = device_of(f, a, ring(b, ways[d]))
        return remote(place, place, b_send.at[f, i, d, kind], b_recv.at[f, i, d, kind], to)

    def landed_two(f, i, d, kind):
        a, b = here[f]
        place = piece(f, ring(a, i), ring(b, ways[1 - d]) if kind == 0 else ring(b, 2), d, kind)
        to = device_of(f, a, ring(b, ways[1 - d]))
        return remote(place, place, b_send.at[f, i, d, kind], b_recv.at[f, i, d, kind], to)

    both = [(f, d) for d in range(2) for f in range(2)]
    for f in range(2):
        arrange(range(f * 25, f * 25 + 25))
        for d in range(2):
            ring_one(f, d, 0).start()
        for d in range(2):
            ring_two(f, 0, d, 0).start()
    for f, d in both:
        landed_one(f, d, 0).wait_recv()
        ring_one(f, d, 1).start()
        for way in range(2):
            ring_two(f, ways[1 - d], way, 0).start()
    for f, d in both:
        landed_two(f, 0, d, 0).wait_recv()
        ring_two(f, 0, d, 1).start()
    for f, d in both:
        landed_one(f, d, 1).wait_recv()
    for f, d in both:
        ring_two(f, 2, d, 0).start()
    for i in (3, 1, 2):
        for f, d in both:
            landed_two(f, i, d, 0).wait_recv()
            ring_two(f, i, d, 1).start()
    for i in range(4):
        for f, d in both:
            landed_two(f, i, d, 1).wait_recv()

    @pl.loop(0, HD)
    def _(h):
        for c in range(10):
            for j in range(8):
                low = w16[j // 2, 2 * (j % 2), h * 10 + c].astype(F32)
                high = w16[j // 2, 2 * (j % 2) + 1, h * 10 + c].astype(F32)
                left = jnp.concatenate([low[:8], high[:8]], axis=0)
                right = jnp.concatenate([low[8:], high[8:]], axis=0)
                w_out[h, j * 16 : (j + 1) * 16, c * 256 : c * 256 + 128] = left.astype(BF)
                w_out[h, j * 16 : (j + 1) * 16, c * 256 + 128 : c * 256 + 256] = right.astype(BF)

    for c in range(CC):
        cot_cross(c).wait_send()
        cot_forward(c).wait_send()
    cot_sibling().wait_send()

    @pl.loop(0, HD)
    def _(h):
        for p in range(3):
            first_x(h, p).wait_send()
            first_z(h, p).wait_send()
            second_x(h, p).wait_send()
            second_z(h, p).wait_send()
        for a in range(3):
            back_own(h, a).wait()
            for p in range(3):
                head_send(h, a, p).wait_send()
                back_copy(h, a, p).wait_send()
                back_recv_copy(h, a, p).wait_recv()

    for f, d in both:
        for kind in range(2):
            ring_one(f, d, kind).wait_send()
            for i in range(4):
                ring_two(f, i, d, kind).wait_send()

    @pl.loop(1, 32)
    def _(k):
        to_owner(k).wait_send()
        from_owner(k).wait_send()

    for i in range(4):
        state_out(i).wait()


def step(q, k, v, cot, w, tile_list, owners, *states):
    any_space = pl.BlockSpec(memory_space=pl.ANY)
    vmem = pl.BlockSpec(memory_space=pltpu.VMEM)
    smem = pl.BlockSpec(memory_space=pltpu.SMEM)
    sems = lambda *shape: pltpu.SemaphoreType.DMA(shape)
    return pl.pallas_call(
        step_kernel,
        out_shape=[jax.ShapeDtypeStruct((TOK, OUTW), BF)] * 3 + [jax.ShapeDtypeStruct((HD, 128, OUTW), BF)]
        + [jax.ShapeDtypeStruct((SL, 128, 128), F32)] * 4,
        in_specs=[any_space] * 5 + [smem] * 2 + [any_space] * 4,
        out_specs=[any_space] * 3 + [vmem] + [any_space] * 4,
        scratch_shapes=[
            pltpu.VMEM((3, HD, LEN, 128), BF),
            pltpu.VMEM((LEN, OUTW), BF),
            pltpu.VMEM((HD * 128, OUTW), BF),
            pltpu.VMEM((HD, LEN, 128), BF),
            pltpu.VMEM((3, HD, LEN, 128), BF),
            pltpu.VMEM((128, LEN), BF),
            pltpu.VMEM((128, LEN), BF),
            pltpu.VMEM((128, LEN), BF),
            pltpu.VMEM((2, 4, LEN, 256), F32),
            pltpu.VMEM((LEN, 128), F32),
            pltpu.VMEM((LEN, 128), F32),
            pltpu.VMEM((HD, 4, 32, 1280), BF),
            pltpu.VMEM((HD, 4, 32, 1280), BF),
            pltpu.VMEM((HD, 3, 32, 1280), BF),
            pltpu.VMEM((HD, 3, 32, 1280), BF),
            pltpu.VMEM((HD, 4, 16, 640), BF),
            pltpu.VMEM((HD, 4, 16, 640), BF),
            pltpu.VMEM((HD, 3, 16, 640), BF),
            pltpu.VMEM((HD, 3, 16, 640), BF),
            pltpu.VMEM((HD * 20, 8, 128), F32),
            sems(2 + 3 * HD),
            sems(HD, 3),
            sems(2 * CC + 1),
            sems(2 * CC + 1),
            *([sems(HD, 3, 3)] * 4),
            *([sems(HD, 3)] * 8),
            pltpu.VMEM((4, SL, 128, 128), F32),
            pltpu.VMEM((32, 4, 16, 128), BF),
            pltpu.VMEM((32, 4, 16, 128), BF),
            pltpu.VMEM((16, 4, 16, 128), BF),
            pltpu.VMEM((32, 4, 16, 128), BF),
            pltpu.VMEM((4, 4, 50, 16, 128), BF),
            sems(4),
            sems(4),
            sems(31),
            sems(31),
            sems(31),
            sems(31),
            sems(2, 2, 2),
            sems(2, 2, 2),
            sems(2, 4, 2, 2),
            sems(2, 4, 2, 2),
            pltpu.VMEM((4, 8, 256), F32),
            pltpu.VMEM((8, 32, 128), jnp.int32),
            pltpu.VMEM((8, 128), jnp.int32),
            pltpu.SMEM((8, 32, 128), jnp.int32),
            pltpu.SMEM((8, 128), jnp.int32),
            sems(2),
        ],
        compiler_params=pltpu.CompilerParams(
            collective_id=0, has_side_effects=True, vmem_limit_bytes=56 * 1024 * 1024
        ),
    )(q, k, v, cot, w, tile_list, owners, *states)


def local(q, k, v, cot, w, tile_list, owners, master, one, two, mean):
    dq, dk, dv, new_w, *states = step(
        q, k, v, cot, w, tile_list, owners[:, 0], master[0], one[0], two[0], mean[0]
    )
    return (dq, dk, dv, new_w.reshape(HD * 128, OUTW), *[s[None] for s in states])


def solution(mesh):
    tokens = P(("dp", "seq"), None)
    state = P("dp", "seq", None, None)
    return jax.shard_map(
        local,
        mesh=mesh,
        in_specs=(tokens,) * 4 + (P("seq", None), P(), P()) + (state,) * 4,
        out_specs=(tokens,) * 3 + (P("seq", None),) + (state,) * 4,
        check_vma=False,
    )
```

```python
import math

import jax
import jax.numpy as jnp
from jax import lax
from jax.experimental import pallas as pl
from jax.experimental.pallas import tpu as pltpu
from jax.sharding import PartitionSpec as P

MESH = pl.DeviceIdType.MESH
BF = jnp.bfloat16
F32 = jnp.float32

learn_rate = 0.001
beta_one = 0.9
beta_two = 0.95
adam_eps = 1e-08
weight_decay = 0.1
ema_keep = 0.99
bias_one = 1.0 - (0.9**50) ** 2
bias_two = 1.0 - (0.95**50) ** 2

HD = 5
TOK = 256
LEN = 1024
OUTW = 2560
SL = 7
NEG = -1e30
SCALE = 1.0 / math.sqrt(128.0)
SCALE2 = SCALE * math.log2(math.e)
BACK_ONE, BACK_TWO = 6, 8
CC = 4


def aligned(value, step):
    return pl.multiple_of(value * step, step)


def remote(src, dst, send, recv, device):
    return pltpu.make_async_remote_copy(
        src_ref=src, dst_ref=dst, send_sem=send, recv_sem=recv, device_id=device, device_id_type=MESH
    )


def dot(a, b):
    return lax.dot_general(a, b, (((1,), (0,)), ((), ())), preferred_element_type=F32)


def dot_nt(a, b):
    return lax.dot_general(a, b, (((1,), (1,)), ((), ())), preferred_element_type=F32)


def place_of():
    dp = lax.axis_index("dp")
    return dp, lax.axis_index("seq"), dp // 8, (dp // 2) % 4, dp % 2


def dp_index(x, z, yh):
    return (x * 4 + z) * 2 + yh


def ring(value, step):
    return lax.rem(value + step, 4)


def adam_step(master_in, first_in, second_in, mean_in, gradient):
    first_out = beta_one * first_in + (1.0 - beta_one) * gradient
    second_out = beta_two * second_in + (1.0 - beta_two) * gradient * gradient
    direction = first_out / bias_one / (jnp.sqrt(second_out / bias_two) + adam_eps)
    master_out = master_in - learn_rate * (direction + weight_decay * master_in)
    mean_out = ema_keep * mean_in + (1.0 - ema_keep) * master_out
    return (master_out, first_out, second_out, mean_out)


def step_kernel(
    q_in, k_in, v_in, cot_in, w_in, tile_list, owners, *refs,
):
    states_in, refs = refs[:4], refs[4:]
    dq_out, dk_out, dv_out, w_out = refs[:4]
    states_out, refs = refs[4:8], refs[8:]
    (
    qkv, cot, w, da, back, kt, vt, att, probs, weights, scale_row, dk_acc, dv_acc,
    gx, gz, r1x, r1z, s2x, s2z, r2x, r2z, sums,
    local_sem, back_local, cot_send, cot_recv, in_send, in_recv, back_send, back_recv,
    x1_send, x1_recv, z1_send, z1_recv, x2_send, x2_recv, z2_send, z2_recv,
    state, tx, rx, pieces, landed, w16,
    state_sem, state_out_sem, t_send, t_recv, n_send, n_recv,
    a_send, a_recv, b_send, b_recv,
    bias, slot_table, block_table, slot_from, block_from, table_sem, w_new, w_sem,
    ) = refs
    dp, me, x, z, yh = place_of()
    sibling = me + 1 - 2 * lax.rem(me, 2)
    across = ring(me, 2)
    corner = ring(sibling, 2)
    peers = [ring(me, p) for p in (1, 2, 3)]
    sources = [ring(me, 4 - p) for p in (1, 2, 3)]
    inputs = (q_in, k_in, v_in)
    outputs = (dq_out, dk_out, dv_out)

    barrier = pltpu.get_barrier_semaphore()
    for t in peers:
        pl.semaphore_signal(barrier, inc=1, device_id=(dp, t), device_id_type=MESH)
    for k in range(1, 32):
        pl.semaphore_signal(barrier, inc=1, device_id=(lax.rem(dp + k, 32), me), device_id_type=MESH)
    pl.semaphore_wait(barrier, 34)

    def rows(s, n=TOK):
        return pl.ds(aligned(s, TOK), n)

    def cot_rows(s, c):
        return pl.ds(pl.multiple_of(s * TOK + c * (TOK // CC), TOK // CC), TOK // CC)

    def cot_cross(c):
        return remote(
            cot_in.at[pl.ds(c * (TOK // CC), TOK // CC)], cot.at[cot_rows(me, c)],
            cot_send.at[c], cot_recv.at[c], (dp, across),
        )

    def cot_sibling():
        return remote(cot_in, cot.at[rows(me)], cot_send.at[CC], cot_recv.at[CC], (dp, sibling))

    def cot_forward(c):
        part = cot.at[cot_rows(across, c)]
        return remote(part, part, cot_send.at[CC + 1 + c], cot_recv.at[CC + 1 + c], (dp, sibling))

    def cot_own():
        return pltpu.make_async_copy(cot_in, cot.at[rows(me)], local_sem.at[0])

    def w_own():
        return pltpu.make_async_copy(w_in, w, local_sem.at[1])

    def head_columns(t, h):
        return pl.ds(pl.multiple_of((t * HD + h) * 128, 128), 128)

    def head_send(h, a, p):
        t = peers[p]
        return remote(
            inputs[a].at[:, head_columns(t, h)], qkv.at[a, h, rows(me)],
            in_send.at[h, a, p], in_recv.at[h, a, p], (dp, t),
        )

    def head_recv(h, a, p):
        part = qkv.at[a, h, rows(sources[p])]
        return remote(part, part, in_send.at[h, a, p], in_recv.at[h, a, p], (dp, sources[p]))

    def head_own(h, a):
        return pltpu.make_async_copy(
            inputs[a].at[:, head_columns(me, h)], qkv.at[a, h, rows(me)], local_sem.at[2 + 3 * h + a]
        )

    def back_copy(h, a, p):
        t = peers[p]
        return remote(
            back.at[a, h, rows(t)], outputs[a].at[:, head_columns(me, h)],
            back_send.at[h, a, p], back_recv.at[h, a, p], (dp, t),
        )

    def back_recv_copy(h, a, p):
        return remote(
            back.at[a, h, rows(sources[p])], outputs[a].at[:, head_columns(sources[p], h)],
            back_send.at[h, a, p], back_recv.at[h, a, p], (dp, sources[p]),
        )

    def back_own(h, a):
        return pltpu.make_async_copy(
            back.at[a, h, rows(me)], outputs[a].at[:, head_columns(me, h)], back_local.at[h, a]
        )

    def state_copy(i):
        return pltpu.make_async_copy(states_in[i], state.at[i], state_sem.at[i])

    def back_start(first, last):
        @pl.loop(first, last)
        def _(unit):
            h, a = unit // 3, lax.rem(unit, 3)
            for i in range(3):

                @pl.when(a == i)
                def _():
                    back_own(h, i).start()
                    for p in range(3):
                        back_copy(h, i, p).start()

    cot_own().start()
    w_own().start()
    for c in range(CC):
        cot_cross(c).start()
    cot_sibling().start()

    @pl.loop(0, HD)
    def _(h):
        for a in range(3):
            head_own(h, a).start()
            for p in range(3):
                head_send(h, a, p).start()

    for i in range(4):
        state_copy(i).start()

    for i in range(8):
        for n in range(8):
            listed = tile_list[i, 0] == n
            for j in range(1, 6):
                listed = listed | (tile_list[i, j] == n)
            low = jnp.where(listed, 0.0, NEG).astype(F32)
            bias[i // 2, n : n + 1, (i % 2) * 128 : (i % 2) * 128 + 128] = jnp.full((1, 128), low, F32)

    lane = lax.broadcasted_iota(jnp.int32, (128, 128), 1)
    row = lax.broadcasted_iota(jnp.int32, (128, 128), 0)

    def put(b, held):
        return jnp.where(lane[:8] == b, owners[me * 100 + b], held)

    owner = lax.fori_loop(0, 100, put, jnp.full((8, 128), -1, jnp.int32))
    owner = jnp.broadcast_to(owner[:1], (128, 128))
    earlier = (owner.T == owner) & (row < lane)
    slot_of = jnp.sum(jnp.where(earlier, 1, 0), axis=0, keepdims=True)
    block_table[...] = jnp.broadcast_to(owner[:1] * 8 + slot_of, (8, 128))
    owned = owner[:32] == row[:32]
    for s in range(SL):
        match = owned & (jnp.broadcast_to(slot_of, (32, 128)) == s)
        block = jnp.sum(jnp.where(match, lane[:32], 0), axis=1, keepdims=True)
        slot_table[s] = jnp.broadcast_to(block, (32, 128))
    count = jnp.sum(jnp.where(owned, 1, 0), axis=1, keepdims=True)
    slot_table[SL] = jnp.broadcast_to(count, (32, 128))
    tables = (
        pltpu.make_async_copy(slot_table, slot_from, table_sem.at[0]),
        pltpu.make_async_copy(block_table, block_from, table_sem.at[1]),
    )
    for table in tables:
        table.start()
    for table in tables:
        table.wait()

    for c in range(CC):
        cot_cross(c).wait_recv()
        cot_forward(c).start()
    cot_own().wait()
    w_own().wait()
    cot_sibling().wait_recv()
    for c in range(CC):
        cot_forward(c).wait_recv()

    @pl.loop(0, 4)
    def _(b):
        d_rows = dot_nt(cot[pl.ds(aligned(b, 256), 256), :], w[...]).astype(BF)
        for h in range(HD):
            da[h, pl.ds(aligned(b, 256), 256), :] = d_rows[:, h * 128 : (h + 1) * 128]

    def scores(h):
        for b in range(4):
            part = slice(b * 256, b * 256 + 256)
            score = dot_nt(qkv[1, h], qkv[0, h, part, :]).reshape(8, 128, 256)
            top = jnp.max(jnp.max(score, axis=1) * SCALE2 + bias[b], axis=0, keepdims=True)
            shift = top - bias[b]
            weight = jnp.exp2(score * SCALE2 - shift[:, None, :]).reshape(LEN, 256)
            total = jnp.sum(weight, axis=0, keepdims=True)
            probs[lax.rem(h, 2), b] = weight
            weights[b] = weight.astype(BF)
            scale_row[lax.rem(h, 2), b] = jnp.broadcast_to(1.0 / total, (8, 256))

    def weight_grad(h):
        vt[...] = qkv[2, h].T
        for b in range(4):
            part = slice(b * 256, b * 256 + 256)
            att[:, part] = (dot(vt[...], weights[b]) * scale_row[lax.rem(h, 2), b, :1]).astype(BF)

        @pl.loop(0, 2)
        def _(c):
            columns = pl.ds(aligned(c, 640), 640)
            grad = dot(att[...], cot[:, columns]).astype(BF)
            for xx in range(4):
                gx[h, xx, :, columns] = grad[xx * 32 : xx * 32 + 32]
            grad = dot(att[...], cot[:, pl.ds(pl.multiple_of(1280 + c * 640, 640), 640)])
            for zz in range(4):
                rows_z = [grad[a * 32 + zz * 8 : a * 32 + zz * 8 + 8] for a in range(4)]
                gz[h, zz, :, columns] = jnp.concatenate(rows_z, axis=0).astype(BF)

    def backward(h):
        kt[...] = qkv[1, h].T
        dk_acc[...] = jnp.zeros_like(dk_acc)
        dv_acc[...] = jnp.zeros_like(dv_acc)
        for b in range(4):
            part = slice(b * 256, b * 256 + 256)
            q_b = qkv[0, h, part, :]
            da_b = da[h, part, :]
            inverse = scale_row[lax.rem(h, 2), b, :1]
            weight = probs[lax.rem(h, 2), b]
            d_prob = dot_nt(qkv[2, h], da_b)
            delta = jnp.sum(weight * d_prob, axis=0, keepdims=True) * inverse
            prob = weight * inverse
            d_score = (prob * (d_prob - delta)).astype(BF)
            back[0, h, part, :] = (dot(kt[...], d_score) * SCALE).T.astype(BF)
            dk_acc[...] += dot(d_score, q_b)
            dv_acc[...] += dot(prob.astype(BF), da_b)

        back[1, h] = (dk_acc[...] * SCALE).astype(BF)
        back[2, h] = dv_acc[...].astype(BF)

    def first_x(h, p):
        t = ring(x, p + 1)
        return remote(gx.at[h, t], r1x.at[h, p], x1_send.at[h, p], x1_recv.at[h, p], (dp_index(t, z, yh), me))

    def first_z(h, p):
        t = ring(z, p + 1)
        return remote(gz.at[h, t], r1z.at[h, p], z1_send.at[h, p], z1_recv.at[h, p], (dp_index(x, t, yh), me))

    def second_z(h, p):
        t = ring(z, p + 1)
        return remote(s2x.at[h, t], r2x.at[h, p], x2_send.at[h, p], x2_recv.at[h, p], (dp_index(x, t, yh), me))

    def second_x(h, p):
        t = ring(x, p + 1)
        return remote(s2z.at[h, t], r2z.at[h, p], z2_send.at[h, p], z2_recv.at[h, p], (dp_index(t, z, yh), me))

    def after_first(h):
        for p in range(3):
            first_x(h, p).wait_recv()
            first_z(h, p).wait_recv()
        total = gx[h, x].astype(F32)
        for p in range(3):
            total = total + r1x[h, p].astype(F32)
        for t in range(4):
            part = total[t * 8 : t * 8 + 8]
            s2x[h, t] = jnp.concatenate([part[:, :640], part[:, 640:]], axis=0).astype(BF)
        total = gz[h, z].astype(F32)
        for p in range(3):
            total = total + r1z[h, p].astype(F32)
        for t in range(4):
            part = total[t * 8 : t * 8 + 8]
            s2z[h, t] = jnp.concatenate([part[:, :640], part[:, 640:]], axis=0).astype(BF)
        for p in range(3):
            second_z(h, p).start()
            second_x(h, p).start()

    def after_second(h):
        for p in range(3):
            second_z(h, p).wait_recv()
            second_x(h, p).wait_recv()
        even = s2x[h, z].astype(F32)
        odd = s2z[h, x].astype(F32)
        for p in range(3):
            even = even + r2x[h, p].astype(F32)
            odd = odd + r2z[h, p].astype(F32)
        for i, total in enumerate((even, odd)):
            for u in range(2):
                for c in range(5):
                    sums[h * 20 + i * 10 + u * 5 + c] = total[u * 8 : u * 8 + 8, c * 128 : c * 128 + 128]

    @pl.loop(0, HD)
    def _(h):
        def arrive(a):
            head_own(h, a).wait()
            for p in range(3):
                head_recv(h, a, p).wait_recv()

        arrive(0)
        arrive(1)

        @pl.when(h == HD - 1)
        def _():
            back_start(0, BACK_ONE)

        scores(h)
        arrive(2)
        weight_grad(h)
        for p in range(3):
            first_x(h, p).start()
            first_z(h, p).start()

        @pl.when(h >= 1)
        def _():
            after_first(h - 1)
            backward(h - 1)
            after_second(h - 1)

    after_first(HD - 1)
    after_second(HD - 1)

    def pack(device):
        tiles = [sums[jnp.clip(slot_from[s, device, 0], 0, HD * 20 - 1)] for s in range(SL)]
        for t in range(4):
            tx[device, t] = jnp.concatenate([tiles[2 * t], tiles[min(2 * t + 1, SL - 1)]], axis=0).astype(BF)

    def to_owner(k):
        device = lax.rem(dp + k, 32)
        return remote(tx.at[device], rx.at[dp], t_send.at[k - 1], t_recv.at[k - 1], (device, me))

    @pl.loop(1, 32)
    def _(k):
        pack(lax.rem(dp + k, 32))
        to_owner(k).start()

    back_start(BACK_ONE, BACK_TWO)
    backward(HD - 1)
    pack(dp)
    rx[dp] = tx[dp]
    for i in range(4):
        state_copy(i).wait()

    @pl.loop(1, 32)
    def _(k):
        to_owner(k).wait_recv()

    def state_out(i):
        return pltpu.make_async_copy(state.at[i], states_out[i], state_out_sem.at[i])

    arrived = rx[...].reshape(16, 2, 4, 16, 128)
    even = None
    for s in range(SL):
        if s % 2 == 0:
            both = arrived[:, 0, s // 2].astype(F32) + arrived[:, 1, s // 2].astype(F32)
        half = both[:, :8] if s % 2 == 0 else both[:, 8:]
        gradient = half.reshape(128, 128) * (1.0 / 32.0)
        before = [state[i, s] for i in range(4)]
        stepped = adam_step(*before, gradient)
        keep = jnp.full((128, 128), slot_from[SL, dp, 0], jnp.int32) > s
        after = [jnp.where(keep, new, old) for new, old in zip(stepped, before)]
        for i in range(4):
            state[i, s] = after[i]
        fresh = after[0].reshape(16, 8, 128)
        if s % 2 == 0:
            even = fresh
        if s % 2 == 1 or s == SL - 1:
            pieces[:, s // 2] = jnp.concatenate([even, fresh], axis=1).astype(BF)
    mine = 4 * x + z

    def from_owner(k):
        device = lax.rem(dp + k, 32)
        return remote(pieces.at[device // 2], landed.at[dp], n_send.at[k - 1], n_recv.at[k - 1], (device, me))

    @pl.loop(1, 32)
    def _(k):
        from_owner(k).start()

    back_start(BACK_TWO, 3 * HD)
    for i in range(4):
        state_out(i).start()
    landed[dp] = pieces[mine]

    @pl.loop(1, 32)
    def _(k):
        from_owner(k).wait_recv()

    def arrange(pairs):
        for pair in pairs:
            halves = []
            for b in (2 * pair, 2 * pair + 1):
                source = jnp.clip(block_from[0, b], 0, 255)
                tile = landed[source // 8, lax.rem(source, 8) // 2].astype(F32)
                odd = jnp.full((8, 128), lax.rem(source, 2), jnp.int32) == 1
                halves.append(jnp.where(odd, tile[8:], tile[:8]))
            w16[x, z, pair] = jnp.concatenate(halves, axis=0).astype(BF)

    here = ((x, z), (z, x))

    def device_of(f, first, second):
        a, b = (first, second) if f == 0 else (second, first)
        return (dp_index(a, b, yh), me)

    def piece(f, first, second, d, kind):
        start, size = f * 25, 25
        if kind == 1:
            start, size = (start, 12) if d == 0 else (start + 12, 13)
        a, b = (first, second) if f == 0 else (second, first)
        return w16.at[a, b, pl.ds(start, size)]

    ways = (1, 3)

    def ring_one(f, d, kind):
        a, b = here[f]
        place = piece(f, a if kind == 0 else ring(a, ways[1 - d]), b, d, kind)
        return remote(place, place, a_send.at[f, d, kind], a_recv.at[f, d, kind], device_of(f, ring(a, ways[d]), b))

    def landed_one(f, d, kind):
        a, b = here[f]
        place = piece(f, ring(a, ways[1 - d]) if kind == 0 else ring(a, 2), b, d, kind)
        return remote(place, place, a_send.at[f, d, kind], a_recv.at[f, d, kind], device_of(f, ring(a, ways[1 - d]), b))

    def ring_two(f, i, d, kind):
        a, b = here[f]
        place = piece(f, ring(a, i), b if kind == 0 else ring(b, ways[1 - d]), d, kind)
        to = device_of(f, a, ring(b, ways[d]))
        return remote(place, place, b_send.at[f, i, d, kind], b_recv.at[f, i, d, kind], to)

    def landed_two(f, i, d, kind):
        a, b = here[f]
        place = piece(f, ring(a, i), ring(b, ways[1 - d]) if kind == 0 else ring(b, 2), d, kind)
        to = device_of(f, a, ring(b, ways[1 - d]))
        return remote(place, place, b_send.at[f, i, d, kind], b_recv.at[f, i, d, kind], to)

    both = [(f, d) for d in range(2) for f in range(2)]
    for f in range(2):
        arrange(range(f * 25, f * 25 + 25))
        for d in range(2):
            ring_one(f, d, 0).start()
        for d in range(2):
            ring_two(f, 0, d, 0).start()
    for f, d in both:
        landed_one(f, d, 0).wait_recv()
        ring_one(f, d, 1).start()
        for way in range(2):
            ring_two(f, ways[1 - d], way, 0).start()
    for f, d in both:
        landed_two(f, 0, d, 0).wait_recv()
        ring_two(f, 0, d, 1).start()
    for f, d in both:
        landed_one(f, d, 1).wait_recv()
    for f, d in both:
        ring_two(f, 2, d, 0).start()
    for i in (3, 1, 2):
        for f, d in both:
            landed_two(f, i, d, 0).wait_recv()
            ring_two(f, i, d, 1).start()
    for i in range(4):
        for f, d in both:
            landed_two(f, i, d, 1).wait_recv()

    def w_copy(h):
        return pltpu.make_async_copy(w_new.at[h], w_out.at[h], w_sem.at[h])

    @pl.loop(0, HD)
    def _(h):
        for c in range(10):
            for j in range(8):
                low = w16[j // 2, 2 * (j % 2), h * 10 + c].astype(F32)
                high = w16[j // 2, 2 * (j % 2) + 1, h * 10 + c].astype(F32)
                left = jnp.concatenate([low[:8], high[:8]], axis=0)
                right = jnp.concatenate([low[8:], high[8:]], axis=0)
                w_new[h, j * 16 : (j + 1) * 16, c * 256 : c * 256 + 128] = left.astype(BF)
                w_new[h, j * 16 : (j + 1) * 16, c * 256 + 128 : c * 256 + 256] = right.astype(BF)
        w_copy(h).start()

    for c in range(CC):
        cot_cross(c).wait_send()
        cot_forward(c).wait_send()
    cot_sibling().wait_send()

    @pl.loop(0, HD)
    def _(h):
        for p in range(3):
            first_x(h, p).wait_send()
            first_z(h, p).wait_send()
            second_x(h, p).wait_send()
            second_z(h, p).wait_send()
        for a in range(3):
            back_own(h, a).wait()
            for p in range(3):
                head_send(h, a, p).wait_send()
                back_copy(h, a, p).wait_send()
                back_recv_copy(h, a, p).wait_recv()

    for f, d in both:
        for kind in range(2):
            ring_one(f, d, kind).wait_send()
            for i in range(4):
                ring_two(f, i, d, kind).wait_send()

    @pl.loop(1, 32)
    def _(k):
        to_owner(k).wait_send()
        from_owner(k).wait_send()

    for i in range(4):
        state_out(i).wait()
    for h in range(HD):
        w_copy(h).wait()


def step(q, k, v, cot, w, tile_list, owners, *states):
    any_space = pl.BlockSpec(memory_space=pl.ANY)
    smem = pl.BlockSpec(memory_space=pltpu.SMEM)
    sems = lambda *shape: pltpu.SemaphoreType.DMA(shape)
    return pl.pallas_call(
        step_kernel,
        out_shape=[jax.ShapeDtypeStruct((TOK, OUTW), BF)] * 3 + [jax.ShapeDtypeStruct((HD, 128, OUTW), BF)]
        + [jax.ShapeDtypeStruct((SL, 128, 128), F32)] * 4,
        in_specs=[any_space] * 5 + [smem] * 2 + [any_space] * 4,
        out_specs=[any_space] * 8,
        scratch_shapes=[
            pltpu.VMEM((3, HD, LEN, 128), BF),
            pltpu.VMEM((LEN, OUTW), BF),
            pltpu.VMEM((HD * 128, OUTW), BF),
            pltpu.VMEM((HD, LEN, 128), BF),
            pltpu.VMEM((3, HD, LEN, 128), BF),
            pltpu.VMEM((128, LEN), BF),
            pltpu.VMEM((128, LEN), BF),
            pltpu.VMEM((128, LEN), BF),
            pltpu.VMEM((2, 4, LEN, 256), F32),
            pltpu.VMEM((4, LEN, 256), BF),
            pltpu.VMEM((2, 4, 8, 256), F32),
            pltpu.VMEM((LEN, 128), F32),
            pltpu.VMEM((LEN, 128), F32),
            pltpu.VMEM((HD, 4, 32, 1280), BF),
            pltpu.VMEM((HD, 4, 32, 1280), BF),
            pltpu.VMEM((HD, 3, 32, 1280), BF),
            pltpu.VMEM((HD, 3, 32, 1280), BF),
            pltpu.VMEM((HD, 4, 16, 640), BF),
            pltpu.VMEM((HD, 4, 16, 640), BF),
            pltpu.VMEM((HD, 3, 16, 640), BF),
            pltpu.VMEM((HD, 3, 16, 640), BF),
            pltpu.VMEM((HD * 20, 8, 128), F32),
            sems(2 + 3 * HD),
            sems(HD, 3),
            sems(2 * CC + 1),
            sems(2 * CC + 1),
            *([sems(HD, 3, 3)] * 4),
            *([sems(HD, 3)] * 8),
            pltpu.VMEM((4, SL, 128, 128), F32),
            pltpu.VMEM((32, 4, 16, 128), BF),
            pltpu.VMEM((32, 4, 16, 128), BF),
            pltpu.VMEM((16, 4, 16, 128), BF),
            pltpu.VMEM((32, 4, 16, 128), BF),
            pltpu.VMEM((4, 4, 50, 16, 128), BF),
            sems(4),
            sems(4),
            sems(31),
            sems(31),
            sems(31),
            sems(31),
            sems(2, 2, 2),
            sems(2, 2, 2),
            sems(2, 4, 2, 2),
            sems(2, 4, 2, 2),
            pltpu.VMEM((4, 8, 256), F32),
            pltpu.VMEM((8, 32, 128), jnp.int32),
            pltpu.VMEM((8, 128), jnp.int32),
            pltpu.SMEM((8, 32, 128), jnp.int32),
            pltpu.SMEM((8, 128), jnp.int32),
            sems(2),
            pltpu.VMEM((HD, 128, OUTW), BF),
            sems(HD),
        ],
        compiler_params=pltpu.CompilerParams(
            collective_id=0, has_side_effects=True, vmem_limit_bytes=56 * 1024 * 1024
        ),
    )(q, k, v, cot, w, tile_list, owners, *states)


def copy_kernel(*refs):
    sources, targets, held, sem = refs[:8], refs[8:16], refs[16:24], refs[24]
    pairs = []
    for source, buffer, target in zip(sources, held, targets):
        half = source.shape[0] // 2
        for part in (pl.ds(0, half), pl.ds(half, source.shape[0] - half)):
            i = len(pairs)
            pairs.append((
                pltpu.make_async_copy(source.at[part], buffer.at[part], sem.at[0, i]),
                pltpu.make_async_copy(buffer.at[part], target.at[part], sem.at[1, i]),
            ))
    for load, _ in pairs:
        load.start()
    for load, store in pairs:
        load.wait()
        store.start()
    for _, store in pairs:
        store.wait()


def copy_out(*arrays):
    space = pl.BlockSpec(memory_space=pltpu.MemorySpace.HBM)
    return pl.pallas_call(
        copy_kernel,
        out_shape=[jax.ShapeDtypeStruct(a.shape, a.dtype) for a in arrays],
        in_specs=[space] * 8,
        out_specs=[space] * 8,
        scratch_shapes=[pltpu.VMEM(a.shape, a.dtype) for a in arrays] + [pltpu.SemaphoreType.DMA((2, 16))],
        compiler_params=pltpu.CompilerParams(vmem_limit_bytes=60 * 1024 * 1024),
    )(*arrays)


def local(q, k, v, cot, w, tile_list, owners, master, one, two, mean):
    results = step(
        q, k, v, cot, w, tile_list, owners[:, 0], master[0], one[0], two[0], mean[0]
    )
    dq, dk, dv, new_w, *states = copy_out(*results)
    return (dq, dk, dv, new_w.reshape(HD * 128, OUTW), *[s[None] for s in states])


def solution(mesh):
    tokens = P(("dp", "seq"), None)
    state = P("dp", "seq", None, None)
    return jax.shard_map(
        local,
        mesh=mesh,
        in_specs=(tokens,) * 4 + (P("seq", None), P(), P()) + (state,) * 4,
        out_specs=(tokens,) * 3 + (P("seq", None),) + (state,) * 4,
        check_vma=False,
    )
```

```python
import math

import jax
import jax.numpy as jnp
from jax import lax
from jax.experimental import pallas as pl
from jax.experimental.pallas import tpu as pltpu
from jax.sharding import PartitionSpec as P

MESH = pl.DeviceIdType.MESH
BF = jnp.bfloat16
F32 = jnp.float32

learn_rate = 0.001
beta_one = 0.9
beta_two = 0.95
adam_eps = 1e-08
weight_decay = 0.1
ema_keep = 0.99
bias_one = 1.0 - (0.9**50) ** 2
bias_two = 1.0 - (0.95**50) ** 2

HD = 5
TOK = 256
LEN = 1024
OUTW = 2560
SL = 7
NEG = -1e30
SCALE = 1.0 / math.sqrt(128.0)
SCALE2 = SCALE * math.log2(math.e)
BACK_ONE, BACK_TWO, BACK_THREE = 4, 5, 7
CC = 4


def aligned(value, step):
    return pl.multiple_of(value * step, step)


def remote(src, dst, send, recv, device):
    return pltpu.make_async_remote_copy(
        src_ref=src, dst_ref=dst, send_sem=send, recv_sem=recv, device_id=device, device_id_type=MESH
    )


def dot(a, b):
    return lax.dot_general(a, b, (((1,), (0,)), ((), ())), preferred_element_type=F32)


def dot_nt(a, b):
    return lax.dot_general(a, b, (((1,), (1,)), ((), ())), preferred_element_type=F32)


def place_of():
    dp = lax.axis_index("dp")
    return dp, lax.axis_index("seq"), dp // 8, (dp // 2) % 4, dp % 2


def dp_index(x, z, yh):
    return (x * 4 + z) * 2 + yh


def ring(value, step):
    return lax.rem(value + step, 4)


def adam_step(master_in, first_in, second_in, mean_in, gradient):
    first_out = beta_one * first_in + (1.0 - beta_one) * gradient
    second_out = beta_two * second_in + (1.0 - beta_two) * gradient * gradient
    direction = first_out / bias_one / (jnp.sqrt(second_out / bias_two) + adam_eps)
    master_out = master_in - learn_rate * (direction + weight_decay * master_in)
    mean_out = ema_keep * mean_in + (1.0 - ema_keep) * master_out
    return (master_out, first_out, second_out, mean_out)


def step_kernel(
    q_in, k_in, v_in, cot_in, w_in, tile_list, owners, *refs,
):
    states_in, refs = refs[:4], refs[4:]
    dq_out, dk_out, dv_out, w_out = refs[:4]
    states_out, refs = refs[4:8], refs[8:]
    (
    qkv, cot, w, da, back, kt, vt, att, probs, weights, scale_row, dk_acc, dv_acc,
    gx, gz, r1x, r1z, s2x, s2z, r2x, r2z, sums,
    local_sem, back_local, cot_send, cot_recv, in_send, in_recv, back_send, back_recv,
    x1_send, x1_recv, z1_send, z1_recv, x2_send, x2_recv, z2_send, z2_recv,
    state, tx, rx, pieces, landed, w16,
    state_sem, state_out_sem, t_send, t_recv, n_send, n_recv,
    a_send, a_recv, b_send, b_recv,
    bias, slot_table, block_table, slot_from, block_from, table_sem, w_new, w_sem,
    ) = refs
    dp, me, x, z, yh = place_of()
    sibling = me + 1 - 2 * lax.rem(me, 2)
    across = ring(me, 2)
    corner = ring(sibling, 2)
    peers = [ring(me, p) for p in (1, 2, 3)]
    sources = [ring(me, 4 - p) for p in (1, 2, 3)]
    inputs = (q_in, k_in, v_in)
    outputs = (dq_out, dk_out, dv_out)

    barrier = pltpu.get_barrier_semaphore()
    for t in peers:
        pl.semaphore_signal(barrier, inc=1, device_id=(dp, t), device_id_type=MESH)
    for k in range(1, 32):
        pl.semaphore_signal(barrier, inc=1, device_id=(lax.rem(dp + k, 32), me), device_id_type=MESH)
    pl.semaphore_wait(barrier, 34)

    def rows(s, n=TOK):
        return pl.ds(aligned(s, TOK), n)

    def cot_rows(s, c):
        return pl.ds(pl.multiple_of(s * TOK + c * (TOK // CC), TOK // CC), TOK // CC)

    def cot_cross(c):
        return remote(
            cot_in.at[pl.ds(c * (TOK // CC), TOK // CC)], cot.at[cot_rows(me, c)],
            cot_send.at[c], cot_recv.at[c], (dp, across),
        )

    def cot_sibling():
        return remote(cot_in, cot.at[rows(me)], cot_send.at[CC], cot_recv.at[CC], (dp, sibling))

    def cot_forward(c):
        part = cot.at[cot_rows(across, c)]
        return remote(part, part, cot_send.at[CC + 1 + c], cot_recv.at[CC + 1 + c], (dp, sibling))

    def cot_own():
        return pltpu.make_async_copy(cot_in, cot.at[rows(me)], local_sem.at[0])

    def w_own():
        return pltpu.make_async_copy(w_in, w, local_sem.at[1])

    def head_columns(t, h):
        return pl.ds(pl.multiple_of((t * HD + h) * 128, 128), 128)

    def head_send(h, a, p):
        t = peers[p]
        return remote(
            inputs[a].at[:, head_columns(t, h)], qkv.at[a, h, rows(me)],
            in_send.at[h, a, p], in_recv.at[h, a, p], (dp, t),
        )

    def head_recv(h, a, p):
        part = qkv.at[a, h, rows(sources[p])]
        return remote(part, part, in_send.at[h, a, p], in_recv.at[h, a, p], (dp, sources[p]))

    def head_own(h, a):
        return pltpu.make_async_copy(
            inputs[a].at[:, head_columns(me, h)], qkv.at[a, h, rows(me)], local_sem.at[2 + 3 * h + a]
        )

    def back_copy(h, a, p):
        t = peers[p]
        return remote(
            back.at[a, h, rows(t)], outputs[a].at[:, head_columns(me, h)],
            back_send.at[h, a, p], back_recv.at[h, a, p], (dp, t),
        )

    def back_recv_copy(h, a, p):
        return remote(
            back.at[a, h, rows(sources[p])], outputs[a].at[:, head_columns(sources[p], h)],
            back_send.at[h, a, p], back_recv.at[h, a, p], (dp, sources[p]),
        )

    def back_own(h, a):
        return pltpu.make_async_copy(
            back.at[a, h, rows(me)], outputs[a].at[:, head_columns(me, h)], back_local.at[h, a]
        )

    def state_copy(i):
        return pltpu.make_async_copy(states_in[i], state.at[i], state_sem.at[i])

    def back_start(first, last):
        @pl.loop(first, last)
        def _(unit):
            h, a = unit // 3, lax.rem(unit, 3)
            for i in range(3):

                @pl.when(a == i)
                def _():
                    back_own(h, i).start()
                    for p in range(3):
                        back_copy(h, i, p).start()

    cot_own().start()
    w_own().start()
    for c in range(CC):
        cot_cross(c).start()
    cot_sibling().start()

    @pl.loop(0, HD)
    def _(h):
        for a in range(3):
            head_own(h, a).start()
            for p in range(3):
                head_send(h, a, p).start()

    for i in range(4):
        state_copy(i).start()

    for i in range(8):
        for n in range(8):
            listed = tile_list[i, 0] == n
            for j in range(1, 6):
                listed = listed | (tile_list[i, j] == n)
            low = jnp.where(listed, 0.0, NEG).astype(F32)
            bias[i // 2, n : n + 1, (i % 2) * 128 : (i % 2) * 128 + 128] = jnp.full((1, 128), low, F32)

    lane = lax.broadcasted_iota(jnp.int32, (128, 128), 1)
    row = lax.broadcasted_iota(jnp.int32, (128, 128), 0)

    def put(b, held):
        return jnp.where(lane[:8] == b, owners[me * 100 + b], held)

    owner = lax.fori_loop(0, 100, put, jnp.full((8, 128), -1, jnp.int32))
    owner = jnp.broadcast_to(owner[:1], (128, 128))
    earlier = (owner.T == owner) & (row < lane)
    slot_of = jnp.sum(jnp.where(earlier, 1, 0), axis=0, keepdims=True)
    block_table[...] = jnp.broadcast_to(owner[:1] * 8 + slot_of, (8, 128))
    owned = owner[:32] == row[:32]
    for s in range(SL):
        match = owned & (jnp.broadcast_to(slot_of, (32, 128)) == s)
        block = jnp.sum(jnp.where(match, lane[:32], 0), axis=1, keepdims=True)
        slot_table[s] = jnp.broadcast_to(block, (32, 128))
    count = jnp.sum(jnp.where(owned, 1, 0), axis=1, keepdims=True)
    slot_table[SL] = jnp.broadcast_to(count, (32, 128))
    tables = (
        pltpu.make_async_copy(slot_table, slot_from, table_sem.at[0]),
        pltpu.make_async_copy(block_table, block_from, table_sem.at[1]),
    )
    for table in tables:
        table.start()
    for table in tables:
        table.wait()

    for c in range(CC):
        cot_cross(c).wait_recv()
        cot_forward(c).start()
    cot_own().wait()
    w_own().wait()
    cot_sibling().wait_recv()
    for c in range(CC):
        cot_forward(c).wait_recv()

    @pl.loop(0, 4)
    def _(b):
        d_rows = dot_nt(cot[pl.ds(aligned(b, 256), 256), :], w[...]).astype(BF)
        for h in range(HD):
            da[h, pl.ds(aligned(b, 256), 256), :] = d_rows[:, h * 128 : (h + 1) * 128]

    def scores(h):
        for b in range(4):
            part = slice(b * 256, b * 256 + 256)
            score = dot_nt(qkv[1, h], qkv[0, h, part, :]).reshape(8, 128, 256)
            top = jnp.max(jnp.max(score, axis=1) * SCALE2 + bias[b], axis=0, keepdims=True)
            shift = top - bias[b]
            weight = jnp.exp2(score * SCALE2 - shift[:, None, :]).reshape(LEN, 256)
            total = jnp.sum(weight, axis=0, keepdims=True)
            probs[lax.rem(h, 2), b] = weight
            weights[b] = weight.astype(BF)
            scale_row[lax.rem(h, 2), b] = jnp.broadcast_to(1.0 / total, (8, 256))

    def weight_grad(h):
        vt[...] = qkv[2, h].T
        for b in range(4):
            part = slice(b * 256, b * 256 + 256)
            att[:, part] = (dot(vt[...], weights[b]) * scale_row[lax.rem(h, 2), b, :1]).astype(BF)

        @pl.loop(0, 2)
        def _(c):
            columns = pl.ds(aligned(c, 640), 640)
            grad = dot(att[...], cot[:, columns]).astype(BF)
            for xx in range(4):
                gx[h, xx, :, columns] = grad[xx * 32 : xx * 32 + 32]
            grad = dot(att[...], cot[:, pl.ds(pl.multiple_of(1280 + c * 640, 640), 640)])
            for zz in range(4):
                rows_z = [grad[a * 32 + zz * 8 : a * 32 + zz * 8 + 8] for a in range(4)]
                gz[h, zz, :, columns] = jnp.concatenate(rows_z, axis=0).astype(BF)

    def backward(h):
        kt[...] = qkv[1, h].T
        dk_acc[...] = jnp.zeros_like(dk_acc)
        dv_acc[...] = jnp.zeros_like(dv_acc)
        for b in range(4):
            part = slice(b * 256, b * 256 + 256)
            q_b = qkv[0, h, part, :]
            da_b = da[h, part, :]
            inverse = scale_row[lax.rem(h, 2), b, :1]
            weight = probs[lax.rem(h, 2), b]
            d_prob = dot_nt(qkv[2, h], da_b)
            delta = jnp.sum(weight * d_prob, axis=0, keepdims=True) * inverse
            prob = weight * inverse
            d_score = (prob * (d_prob - delta)).astype(BF)
            back[0, h, part, :] = (dot(kt[...], d_score) * SCALE).T.astype(BF)
            dk_acc[...] += dot(d_score, q_b)
            dv_acc[...] += dot(prob.astype(BF), da_b)

        back[1, h] = (dk_acc[...] * SCALE).astype(BF)
        back[2, h] = dv_acc[...].astype(BF)

    def first_x(h, p):
        t = ring(x, p + 1)
        return remote(gx.at[h, t], r1x.at[h, p], x1_send.at[h, p], x1_recv.at[h, p], (dp_index(t, z, yh), me))

    def first_z(h, p):
        t = ring(z, p + 1)
        return remote(gz.at[h, t], r1z.at[h, p], z1_send.at[h, p], z1_recv.at[h, p], (dp_index(x, t, yh), me))

    def second_z(h, p):
        t = ring(z, p + 1)
        return remote(s2x.at[h, t], r2x.at[h, p], x2_send.at[h, p], x2_recv.at[h, p], (dp_index(x, t, yh), me))

    def second_x(h, p):
        t = ring(x, p + 1)
        return remote(s2z.at[h, t], r2z.at[h, p], z2_send.at[h, p], z2_recv.at[h, p], (dp_index(t, z, yh), me))

    def after_first(h):
        for p in range(3):
            first_x(h, p).wait_recv()
            first_z(h, p).wait_recv()
        total = gx[h, x].astype(F32)
        for p in range(3):
            total = total + r1x[h, p].astype(F32)
        for t in range(4):
            part = total[t * 8 : t * 8 + 8]
            s2x[h, t] = jnp.concatenate([part[:, :640], part[:, 640:]], axis=0).astype(BF)
        total = gz[h, z].astype(F32)
        for p in range(3):
            total = total + r1z[h, p].astype(F32)
        for t in range(4):
            part = total[t * 8 : t * 8 + 8]
            s2z[h, t] = jnp.concatenate([part[:, :640], part[:, 640:]], axis=0).astype(BF)
        for p in range(3):
            second_z(h, p).start()
            second_x(h, p).start()

    def after_second(h):
        for p in range(3):
            second_z(h, p).wait_recv()
            second_x(h, p).wait_recv()
        even = s2x[h, z].astype(F32)
        odd = s2z[h, x].astype(F32)
        for p in range(3):
            even = even + r2x[h, p].astype(F32)
            odd = odd + r2z[h, p].astype(F32)
        for i, total in enumerate((even, odd)):
            for u in range(2):
                for c in range(5):
                    sums[h * 20 + i * 10 + u * 5 + c] = total[u * 8 : u * 8 + 8, c * 128 : c * 128 + 128]

    @pl.loop(0, HD)
    def _(h):
        def arrive(a):
            head_own(h, a).wait()
            for p in range(3):
                head_recv(h, a, p).wait_recv()

        arrive(0)
        arrive(1)

        @pl.when(h == HD - 1)
        def _():
            back_start(0, BACK_ONE)

        scores(h)
        arrive(2)
        weight_grad(h)
        for p in range(3):
            first_x(h, p).start()
            first_z(h, p).start()

        @pl.when(h >= 1)
        def _():
            after_first(h - 1)
            backward(h - 1)
            after_second(h - 1)

    after_first(HD - 1)
    back_start(BACK_ONE, BACK_TWO)
    after_second(HD - 1)

    def pack(device):
        tiles = [sums[jnp.clip(slot_from[s, device, 0], 0, HD * 20 - 1)] for s in range(SL)]
        for t in range(4):
            tx[device, t] = jnp.concatenate([tiles[2 * t], tiles[min(2 * t + 1, SL - 1)]], axis=0).astype(BF)

    def to_owner(k):
        device = lax.rem(dp + k, 32)
        return remote(tx.at[device], rx.at[dp], t_send.at[k - 1], t_recv.at[k - 1], (device, me))

    @pl.loop(0, 31)
    def _(i):
        k = jnp.where(i < 16, 2 * i + 1, 2 * i - 30)
        pack(lax.rem(dp + k, 32))
        to_owner(k).start()

    back_start(BACK_TWO, BACK_THREE)
    backward(HD - 1)
    pack(dp)
    rx[dp] = tx[dp]
    for i in range(4):
        state_copy(i).wait()

    @pl.loop(1, 32)
    def _(k):
        to_owner(k).wait_recv()

    def state_out(i):
        return pltpu.make_async_copy(state.at[i], states_out[i], state_out_sem.at[i])

    arrived = rx[...].reshape(16, 2, 4, 16, 128)
    even = None
    for s in range(SL):
        if s % 2 == 0:
            both = arrived[:, 0, s // 2].astype(F32) + arrived[:, 1, s // 2].astype(F32)
        half = both[:, :8] if s % 2 == 0 else both[:, 8:]
        gradient = half.reshape(128, 128) * (1.0 / 32.0)
        before = [state[i, s] for i in range(4)]
        stepped = adam_step(*before, gradient)
        keep = jnp.full((128, 128), slot_from[SL, dp, 0], jnp.int32) > s
        after = [jnp.where(keep, new, old) for new, old in zip(stepped, before)]
        for i in range(4):
            state[i, s] = after[i]
        fresh = after[0].reshape(16, 8, 128)
        if s % 2 == 0:
            even = fresh
        if s % 2 == 1 or s == SL - 1:
            pieces[:, s // 2] = jnp.concatenate([even, fresh], axis=1).astype(BF)
    mine = 4 * x + z

    def from_owner(k):
        device = lax.rem(dp + k, 32)
        return remote(pieces.at[device // 2], landed.at[dp], n_send.at[k - 1], n_recv.at[k - 1], (device, me))

    @pl.loop(0, 31)
    def _(i):
        from_owner(jnp.where(i < 16, 2 * i + 1, 2 * i - 30)).start()

    back_start(BACK_THREE, 3 * HD)
    for i in range(4):
        state_out(i).start()
    landed[dp] = pieces[mine]

    @pl.loop(1, 32)
    def _(k):
        from_owner(k).wait_recv()

    def arrange(pairs):
        for pair in pairs:
            halves = []
            for b in (2 * pair, 2 * pair + 1):
                source = jnp.clip(block_from[0, b], 0, 255)
                tile = landed[source // 8, lax.rem(source, 8) // 2].astype(F32)
                odd = jnp.full((8, 128), lax.rem(source, 2), jnp.int32) == 1
                halves.append(jnp.where(odd, tile[8:], tile[:8]))
            w16[x, z, pair] = jnp.concatenate(halves, axis=0).astype(BF)

    here = ((x, z), (z, x))

    def device_of(f, first, second):
        a, b = (first, second) if f == 0 else (second, first)
        return (dp_index(a, b, yh), me)

    def piece(f, first, second, d, kind):
        start, size = f * 25, 25
        if kind == 1:
            start, size = (start, 12) if d == 0 else (start + 12, 13)
        a, b = (first, second) if f == 0 else (second, first)
        return w16.at[a, b, pl.ds(start, size)]

    ways = (1, 3)

    def ring_one(f, d, kind):
        a, b = here[f]
        place = piece(f, a if kind == 0 else ring(a, ways[1 - d]), b, d, kind)
        return remote(place, place, a_send.at[f, d, kind], a_recv.at[f, d, kind], device_of(f, ring(a, ways[d]), b))

    def landed_one(f, d, kind):
        a, b = here[f]
        place = piece(f, ring(a, ways[1 - d]) if kind == 0 else ring(a, 2), b, d, kind)
        return remote(place, place, a_send.at[f, d, kind], a_recv.at[f, d, kind], device_of(f, ring(a, ways[1 - d]), b))

    def ring_two(f, i, d, kind):
        a, b = here[f]
        place = piece(f, ring(a, i), b if kind == 0 else ring(b, ways[1 - d]), d, kind)
        to = device_of(f, a, ring(b, ways[d]))
        return remote(place, place, b_send.at[f, i, d, kind], b_recv.at[f, i, d, kind], to)

    def landed_two(f, i, d, kind):
        a, b = here[f]
        place = piece(f, ring(a, i), ring(b, ways[1 - d]) if kind == 0 else ring(b, 2), d, kind)
        to = device_of(f, a, ring(b, ways[1 - d]))
        return remote(place, place, b_send.at[f, i, d, kind], b_recv.at[f, i, d, kind], to)

    both = [(f, d) for d in range(2) for f in range(2)]
    for f in range(2):
        arrange(range(f * 25, f * 25 + 25))
        for d in range(2):
            ring_one(f, d, 0).start()
        for d in range(2):
            ring_two(f, 0, d, 0).start()
    for f, d in both:
        landed_one(f, d, 0).wait_recv()
        ring_one(f, d, 1).start()
        for way in range(2):
            ring_two(f, ways[1 - d], way, 0).start()
    for f, d in both:
        landed_two(f, 0, d, 0).wait_recv()
        ring_two(f, 0, d, 1).start()
    for f, d in both:
        landed_one(f, d, 1).wait_recv()
    for f, d in both:
        ring_two(f, 2, d, 0).start()
    for i in (3, 1, 2):
        for f, d in both:
            landed_two(f, i, d, 0).wait_recv()
            ring_two(f, i, d, 1).start()

    def w_copy(h):
        return pltpu.make_async_copy(w_new.at[h], w_out.at[h], w_sem.at[h])

    def rows_of(first, pairs):
        for pair in pairs:
            h, c = pair // 10, pair % 10
            for m in range(2):
                low = w16[first, 2 * m, pair].astype(F32)
                high = w16[first, 2 * m + 1, pair].astype(F32)
                place = pl.ds(pl.multiple_of(first * 32 + m * 16, 16), 16)
                left = jnp.concatenate([low[:8], high[:8]], axis=0)
                right = jnp.concatenate([low[8:], high[8:]], axis=0)
                w_new[h, place, c * 256 : c * 256 + 128] = left.astype(BF)
                w_new[h, place, c * 256 + 128 : c * 256 + 256] = right.astype(BF)

    for i in (0, 3, 1, 2):
        for d in range(2):
            landed_two(0, i, d, 1).wait_recv()
        rows_of(ring(x, i), range(25))
    for h in range(2):
        w_copy(h).start()
    for i in range(4):
        for d in range(2):
            landed_two(1, i, d, 1).wait_recv()

    @pl.loop(0, 4)
    def _(first):
        rows_of(first, range(25, 50))

    for h in range(2, HD):
        w_copy(h).start()

    for c in range(CC):
        cot_cross(c).wait_send()
        cot_forward(c).wait_send()
    cot_sibling().wait_send()

    @pl.loop(0, HD)
    def _(h):
        for p in range(3):
            first_x(h, p).wait_send()
            first_z(h, p).wait_send()
            second_x(h, p).wait_send()
            second_z(h, p).wait_send()
        for a in range(3):
            back_own(h, a).wait()
            for p in range(3):
                head_send(h, a, p).wait_send()
                back_copy(h, a, p).wait_send()
                back_recv_copy(h, a, p).wait_recv()

    for f, d in both:
        for kind in range(2):
            ring_one(f, d, kind).wait_send()
            for i in range(4):
                ring_two(f, i, d, kind).wait_send()

    @pl.loop(1, 32)
    def _(k):
        to_owner(k).wait_send()
        from_owner(k).wait_send()

    for i in range(4):
        state_out(i).wait()
    for h in range(HD):
        w_copy(h).wait()


def step(q, k, v, cot, w, tile_list, owners, *states):
    any_space = pl.BlockSpec(memory_space=pl.ANY)
    smem = pl.BlockSpec(memory_space=pltpu.SMEM)
    sems = lambda *shape: pltpu.SemaphoreType.DMA(shape)
    return pl.pallas_call(
        step_kernel,
        out_shape=[jax.ShapeDtypeStruct((TOK, OUTW), BF)] * 3 + [jax.ShapeDtypeStruct((HD, 128, OUTW), BF)]
        + [jax.ShapeDtypeStruct((SL, 128, 128), F32)] * 4,
        in_specs=[any_space] * 5 + [smem] * 2 + [any_space] * 4,
        out_specs=[any_space] * 8,
        scratch_shapes=[
            pltpu.VMEM((3, HD, LEN, 128), BF),
            pltpu.VMEM((LEN, OUTW), BF),
            pltpu.VMEM((HD * 128, OUTW), BF),
            pltpu.VMEM((HD, LEN, 128), BF),
            pltpu.VMEM((3, HD, LEN, 128), BF),
            pltpu.VMEM((128, LEN), BF),
            pltpu.VMEM((128, LEN), BF),
            pltpu.VMEM((128, LEN), BF),
            pltpu.VMEM((2, 4, LEN, 256), F32),
            pltpu.VMEM((4, LEN, 256), BF),
            pltpu.VMEM((2, 4, 8, 256), F32),
            pltpu.VMEM((LEN, 128), F32),
            pltpu.VMEM((LEN, 128), F32),
            pltpu.VMEM((HD, 4, 32, 1280), BF),
            pltpu.VMEM((HD, 4, 32, 1280), BF),
            pltpu.VMEM((HD, 3, 32, 1280), BF),
            pltpu.VMEM((HD, 3, 32, 1280), BF),
            pltpu.VMEM((HD, 4, 16, 640), BF),
            pltpu.VMEM((HD, 4, 16, 640), BF),
            pltpu.VMEM((HD, 3, 16, 640), BF),
            pltpu.VMEM((HD, 3, 16, 640), BF),
            pltpu.VMEM((HD * 20, 8, 128), F32),
            sems(2 + 3 * HD),
            sems(HD, 3),
            sems(2 * CC + 1),
            sems(2 * CC + 1),
            *([sems(HD, 3, 3)] * 4),
            *([sems(HD, 3)] * 8),
            pltpu.VMEM((4, SL, 128, 128), F32),
            pltpu.VMEM((32, 4, 16, 128), BF),
            pltpu.VMEM((32, 4, 16, 128), BF),
            pltpu.VMEM((16, 4, 16, 128), BF),
            pltpu.VMEM((32, 4, 16, 128), BF),
            pltpu.VMEM((4, 4, 50, 16, 128), BF),
            sems(4),
            sems(4),
            sems(31),
            sems(31),
            sems(31),
            sems(31),
            sems(2, 2, 2),
            sems(2, 2, 2),
            sems(2, 4, 2, 2),
            sems(2, 4, 2, 2),
            pltpu.VMEM((4, 8, 256), F32),
            pltpu.VMEM((8, 32, 128), jnp.int32),
            pltpu.VMEM((8, 128), jnp.int32),
            pltpu.SMEM((8, 32, 128), jnp.int32),
            pltpu.SMEM((8, 128), jnp.int32),
            sems(2),
            pltpu.VMEM((HD, 128, OUTW), BF),
            sems(HD),
        ],
        compiler_params=pltpu.CompilerParams(
            collective_id=0, has_side_effects=True, vmem_limit_bytes=56 * 1024 * 1024
        ),
    )(q, k, v, cot, w, tile_list, owners, *states)


def copy_kernel(*refs):
    sources, targets, held, sem = refs[:8], refs[8:16], refs[16:24], refs[24]
    pairs = []
    for source, buffer, target in zip(sources, held, targets):
        half = source.shape[0] // 2
        for part in (pl.ds(0, half), pl.ds(half, source.shape[0] - half)):
            i = len(pairs)
            pairs.append((
                pltpu.make_async_copy(source.at[part], buffer.at[part], sem.at[0, i]),
                pltpu.make_async_copy(buffer.at[part], target.at[part], sem.at[1, i]),
            ))
    for load, _ in pairs:
        load.start()
    for load, store in pairs:
        load.wait()
        store.start()
    for _, store in pairs:
        store.wait()


def copy_out(*arrays):
    space = pl.BlockSpec(memory_space=pltpu.MemorySpace.HBM)
    return pl.pallas_call(
        copy_kernel,
        out_shape=[jax.ShapeDtypeStruct(a.shape, a.dtype) for a in arrays],
        in_specs=[space] * 8,
        out_specs=[space] * 8,
        scratch_shapes=[pltpu.VMEM(a.shape, a.dtype) for a in arrays] + [pltpu.SemaphoreType.DMA((2, 16))],
        compiler_params=pltpu.CompilerParams(vmem_limit_bytes=60 * 1024 * 1024),
    )(*arrays)


def local(q, k, v, cot, w, tile_list, owners, master, one, two, mean):
    results = step(
        q, k, v, cot, w, tile_list, owners[:, 0], master[0], one[0], two[0], mean[0]
    )
    dq, dk, dv, new_w, *states = copy_out(*results)
    return (dq, dk, dv, new_w.reshape(HD * 128, OUTW), *[s[None] for s in states])


def solution(mesh):
    tokens = P(("dp", "seq"), None)
    state = P("dp", "seq", None, None)
    return jax.shard_map(
        local,
        mesh=mesh,
        in_specs=(tokens,) * 4 + (P("seq", None), P(), P()) + (state,) * 4,
        out_specs=(tokens,) * 3 + (P("seq", None),) + (state,) * 4,
        check_vma=False,
    )
```

```python
import math

import jax
import jax.numpy as jnp
from jax import lax
from jax.experimental import pallas as pl
from jax.experimental.pallas import tpu as pltpu
from jax.sharding import PartitionSpec as P

MESH = pl.DeviceIdType.MESH
BF = jnp.bfloat16
F32 = jnp.float32

learn_rate = 0.001
beta_one = 0.9
beta_two = 0.95
adam_eps = 1e-08
weight_decay = 0.1
ema_keep = 0.99
bias_one = 1.0 - (0.9**50) ** 2
bias_two = 1.0 - (0.95**50) ** 2

HD = 5
TOK = 256
LEN = 1024
OUTW = 2560
SL = 7
NEG = -1e30
SCALE = 1.0 / math.sqrt(128.0)
SCALE2 = SCALE * math.log2(math.e)
BACK_ONE, BACK_TWO, BACK_THREE = 4, 5, 7
CC = 4


def aligned(value, step):
    return pl.multiple_of(value * step, step)


def remote(src, dst, send, recv, device):
    return pltpu.make_async_remote_copy(
        src_ref=src, dst_ref=dst, send_sem=send, recv_sem=recv, device_id=device, device_id_type=MESH
    )


def dot(a, b):
    return lax.dot_general(a, b, (((1,), (0,)), ((), ())), preferred_element_type=F32)


def dot_nt(a, b):
    return lax.dot_general(a, b, (((1,), (1,)), ((), ())), preferred_element_type=F32)


def place_of():
    dp = lax.axis_index("dp")
    return dp, lax.axis_index("seq"), dp // 8, (dp // 2) % 4, dp % 2


def dp_index(x, z, yh):
    return (x * 4 + z) * 2 + yh


def ring(value, step):
    return lax.rem(value + step, 4)


def adam_step(master_in, first_in, second_in, mean_in, gradient):
    first_out = beta_one * first_in + (1.0 - beta_one) * gradient
    second_out = beta_two * second_in + (1.0 - beta_two) * gradient * gradient
    direction = first_out / bias_one / (jnp.sqrt(second_out / bias_two) + adam_eps)
    master_out = master_in - learn_rate * (direction + weight_decay * master_in)
    mean_out = ema_keep * mean_in + (1.0 - ema_keep) * master_out
    return (master_out, first_out, second_out, mean_out)


def step_kernel(
    q_in, k_in, v_in, cot_in, w_in, tile_list, owners, *refs,
):
    states_in, refs = refs[:4], refs[4:]
    dq_out, dk_out, dv_out, w_out = refs[:4]
    states_out, refs = refs[4:8], refs[8:]
    (
    qkv, cot, w, da, back, kt, vt, att, probs, weights, scale_row, dk_acc, dv_acc,
    gx, gz, r1x, r1z, s2x, s2z, r2x, r2z, sums,
    local_sem, back_local, cot_send, cot_recv, in_send, in_recv, back_send, back_recv,
    x1_send, x1_recv, z1_send, z1_recv, x2_send, x2_recv, z2_send, z2_recv,
    state, tx, rx, pieces, landed, w16,
    state_sem, state_out_sem, t_send, t_recv, n_send, n_recv,
    a_send, a_recv, b_send, b_recv,
    bias, slot_table, block_table, slot_from, block_from, table_sem, w_new, w_sem, half_sum, half_out, half_in, y_send, y_recv,
    ) = refs
    dp, me, x, z, yh = place_of()
    sibling = me + 1 - 2 * lax.rem(me, 2)
    across = ring(me, 2)
    corner = ring(sibling, 2)
    peers = [ring(me, p) for p in (1, 2, 3)]
    sources = [ring(me, 4 - p) for p in (1, 2, 3)]
    inputs = (q_in, k_in, v_in)
    outputs = (dq_out, dk_out, dv_out)

    barrier = pltpu.get_barrier_semaphore()
    for t in peers:
        pl.semaphore_signal(barrier, inc=1, device_id=(dp, t), device_id_type=MESH)
    for k in range(1, 32):
        pl.semaphore_signal(barrier, inc=1, device_id=(lax.rem(dp + k, 32), me), device_id_type=MESH)
    pl.semaphore_wait(barrier, 34)

    def rows(s, n=TOK):
        return pl.ds(aligned(s, TOK), n)

    def cot_rows(s, c):
        return pl.ds(pl.multiple_of(s * TOK + c * (TOK // CC), TOK // CC), TOK // CC)

    def cot_cross(c):
        return remote(
            cot_in.at[pl.ds(c * (TOK // CC), TOK // CC)], cot.at[cot_rows(me, c)],
            cot_send.at[c], cot_recv.at[c], (dp, across),
        )

    def cot_sibling():
        return remote(cot_in, cot.at[rows(me)], cot_send.at[CC], cot_recv.at[CC], (dp, sibling))

    def cot_forward(c):
        part = cot.at[cot_rows(across, c)]
        return remote(part, part, cot_send.at[CC + 1 + c], cot_recv.at[CC + 1 + c], (dp, sibling))

    def cot_own():
        return pltpu.make_async_copy(cot_in, cot.at[rows(me)], local_sem.at[0])

    def w_own():
        return pltpu.make_async_copy(w_in, w, local_sem.at[1])

    def head_columns(t, h):
        return pl.ds(pl.multiple_of((t * HD + h) * 128, 128), 128)

    def head_send(h, a, p):
        t = peers[p]
        return remote(
            inputs[a].at[:, head_columns(t, h)], qkv.at[a, h, rows(me)],
            in_send.at[h, a, p], in_recv.at[h, a, p], (dp, t),
        )

    def head_recv(h, a, p):
        part = qkv.at[a, h, rows(sources[p])]
        return remote(part, part, in_send.at[h, a, p], in_recv.at[h, a, p], (dp, sources[p]))

    def head_own(h, a):
        return pltpu.make_async_copy(
            inputs[a].at[:, head_columns(me, h)], qkv.at[a, h, rows(me)], local_sem.at[2 + 3 * h + a]
        )

    def back_copy(h, a, p):
        t = peers[p]
        return remote(
            back.at[a, h, rows(t)], outputs[a].at[:, head_columns(me, h)],
            back_send.at[h, a, p], back_recv.at[h, a, p], (dp, t),
        )

    def back_recv_copy(h, a, p):
        return remote(
            back.at[a, h, rows(sources[p])], outputs[a].at[:, head_columns(sources[p], h)],
            back_send.at[h, a, p], back_recv.at[h, a, p], (dp, sources[p]),
        )

    def back_own(h, a):
        return pltpu.make_async_copy(
            back.at[a, h, rows(me)], outputs[a].at[:, head_columns(me, h)], back_local.at[h, a]
        )

    def state_copy(i):
        return pltpu.make_async_copy(states_in[i], state.at[i], state_sem.at[i])

    def back_start(first, last):
        @pl.loop(first, last)
        def _(unit):
            h, a = unit // 3, lax.rem(unit, 3)
            for i in range(3):

                @pl.when(a == i)
                def _():
                    back_own(h, i).start()
                    for p in range(3):
                        back_copy(h, i, p).start()

    cot_own().start()
    w_own().start()
    for c in range(CC):
        cot_cross(c).start()
    cot_sibling().start()

    @pl.loop(0, HD)
    def _(h):
        for a in range(3):
            head_own(h, a).start()
            for p in range(3):
                head_send(h, a, p).start()

    for i in range(4):
        state_copy(i).start()

    for i in range(8):
        for n in range(8):
            listed = tile_list[i, 0] == n
            for j in range(1, 6):
                listed = listed | (tile_list[i, j] == n)
            low = jnp.where(listed, 0.0, NEG).astype(F32)
            bias[i // 2, n : n + 1, (i % 2) * 128 : (i % 2) * 128 + 128] = jnp.full((1, 128), low, F32)

    lane = lax.broadcasted_iota(jnp.int32, (128, 128), 1)
    row = lax.broadcasted_iota(jnp.int32, (128, 128), 0)

    def put(b, held):
        return jnp.where(lane[:8] == b, owners[me * 100 + b], held)

    owner = lax.fori_loop(0, 100, put, jnp.full((8, 128), -1, jnp.int32))
    owner = jnp.broadcast_to(owner[:1], (128, 128))
    earlier = (owner.T == owner) & (row < lane)
    slot_of = jnp.sum(jnp.where(earlier, 1, 0), axis=0, keepdims=True)
    block_table[...] = jnp.broadcast_to(owner[:1] * 8 + slot_of, (8, 128))
    owned = owner[:32] == row[:32]
    for s in range(SL):
        match = owned & (jnp.broadcast_to(slot_of, (32, 128)) == s)
        block = jnp.sum(jnp.where(match, lane[:32], 0), axis=1, keepdims=True)
        slot_table[s] = jnp.broadcast_to(block, (32, 128))
    count = jnp.sum(jnp.where(owned, 1, 0), axis=1, keepdims=True)
    slot_table[SL] = jnp.broadcast_to(count, (32, 128))
    tables = (
        pltpu.make_async_copy(slot_table, slot_from, table_sem.at[0]),
        pltpu.make_async_copy(block_table, block_from, table_sem.at[1]),
    )
    for table in tables:
        table.start()
    for table in tables:
        table.wait()

    for c in range(CC):
        cot_cross(c).wait_recv()
        cot_forward(c).start()
    cot_own().wait()
    w_own().wait()
    cot_sibling().wait_recv()
    for c in range(CC):
        cot_forward(c).wait_recv()

    @pl.loop(0, 4)
    def _(b):
        d_rows = dot_nt(cot[pl.ds(aligned(b, 256), 256), :], w[...]).astype(BF)
        for h in range(HD):
            da[h, pl.ds(aligned(b, 256), 256), :] = d_rows[:, h * 128 : (h + 1) * 128]

    def scores(h):
        for b in range(4):
            part = slice(b * 256, b * 256 + 256)
            score = dot_nt(qkv[1, h], qkv[0, h, part, :]).reshape(8, 128, 256)
            top = jnp.max(jnp.max(score, axis=1) * SCALE2 + bias[b], axis=0, keepdims=True)
            shift = top - bias[b]
            weight = jnp.exp2(score * SCALE2 - shift[:, None, :]).reshape(LEN, 256)
            total = jnp.sum(weight, axis=0, keepdims=True)
            probs[lax.rem(h, 2), b] = weight
            weights[b] = weight.astype(BF)
            scale_row[lax.rem(h, 2), b] = jnp.broadcast_to(1.0 / total, (8, 256))

    def weight_grad(h):
        vt[...] = qkv[2, h].T
        for b in range(4):
            part = slice(b * 256, b * 256 + 256)
            att[:, part] = (dot(vt[...], weights[b]) * scale_row[lax.rem(h, 2), b, :1]).astype(BF)

        @pl.loop(0, 2)
        def _(c):
            columns = pl.ds(aligned(c, 640), 640)
            grad = dot(att[...], cot[:, columns]).astype(BF)
            for xx in range(4):
                gx[h, xx, :, columns] = grad[xx * 32 : xx * 32 + 32]
            grad = dot(att[...], cot[:, pl.ds(pl.multiple_of(1280 + c * 640, 640), 640)])
            for zz in range(4):
                rows_z = [grad[a * 32 + zz * 8 : a * 32 + zz * 8 + 8] for a in range(4)]
                gz[h, zz, :, columns] = jnp.concatenate(rows_z, axis=0).astype(BF)

    def backward(h):
        kt[...] = qkv[1, h].T
        dk_acc[...] = jnp.zeros_like(dk_acc)
        dv_acc[...] = jnp.zeros_like(dv_acc)
        for b in range(4):
            part = slice(b * 256, b * 256 + 256)
            q_b = qkv[0, h, part, :]
            da_b = da[h, part, :]
            inverse = scale_row[lax.rem(h, 2), b, :1]
            weight = probs[lax.rem(h, 2), b]
            d_prob = dot_nt(qkv[2, h], da_b)
            delta = jnp.sum(weight * d_prob, axis=0, keepdims=True) * inverse
            prob = weight * inverse
            d_score = (prob * (d_prob - delta)).astype(BF)
            back[0, h, part, :] = (dot(kt[...], d_score) * SCALE).T.astype(BF)
            dk_acc[...] += dot(d_score, q_b)
            dv_acc[...] += dot(prob.astype(BF), da_b)

        back[1, h] = (dk_acc[...] * SCALE).astype(BF)
        back[2, h] = dv_acc[...].astype(BF)

    def first_x(h, p):
        t = ring(x, p + 1)
        return remote(gx.at[h, t], r1x.at[h, p], x1_send.at[h, p], x1_recv.at[h, p], (dp_index(t, z, yh), me))

    def first_z(h, p):
        t = ring(z, p + 1)
        return remote(gz.at[h, t], r1z.at[h, p], z1_send.at[h, p], z1_recv.at[h, p], (dp_index(x, t, yh), me))

    def second_z(h, p):
        t = ring(z, p + 1)
        return remote(s2x.at[h, t], r2x.at[h, p], x2_send.at[h, p], x2_recv.at[h, p], (dp_index(x, t, yh), me))

    def second_x(h, p):
        t = ring(x, p + 1)
        return remote(s2z.at[h, t], r2z.at[h, p], z2_send.at[h, p], z2_recv.at[h, p], (dp_index(t, z, yh), me))

    def other_half(h):
        return remote(half_out.at[h], half_in.at[h], y_send.at[h], y_recv.at[h], (dp_index(x, z, 1 - yh), me))

    def after_first(h):
        for p in range(3):
            first_x(h, p).wait_recv()
            first_z(h, p).wait_recv()
        total = gx[h, x].astype(F32)
        for p in range(3):
            total = total + r1x[h, p].astype(F32)
        for t in range(4):
            part = total[t * 8 : t * 8 + 8]
            s2x[h, t] = jnp.concatenate([part[:, :640], part[:, 640:]], axis=0).astype(BF)
        total = gz[h, z].astype(F32)
        for p in range(3):
            total = total + r1z[h, p].astype(F32)
        for t in range(4):
            part = total[t * 8 : t * 8 + 8]
            s2z[h, t] = jnp.concatenate([part[:, :640], part[:, 640:]], axis=0).astype(BF)
        for p in range(3):
            second_z(h, p).start()
            second_x(h, p).start()

    def after_second(h):
        for p in range(3):
            second_z(h, p).wait_recv()
            second_x(h, p).wait_recv()
        even = s2x[h, z].astype(F32)
        odd = s2z[h, x].astype(F32)
        for p in range(3):
            even = even + r2x[h, p].astype(F32)
            odd = odd + r2z[h, p].astype(F32)
        for i, total in enumerate((even, odd)):
            half_sum[h, i] = total
            half_out[h, i] = total.astype(BF)
        other_half(h).start()

    def after_third(h):
        other_half(h).wait_recv()
        for i in range(2):
            total = half_sum[h, i] + half_in[h, i].astype(F32)
            for u in range(2):
                for c in range(5):
                    sums[h * 20 + i * 10 + u * 5 + c] = total[u * 8 : u * 8 + 8, c * 128 : c * 128 + 128]

    @pl.loop(0, HD)
    def _(h):
        def arrive(a):
            head_own(h, a).wait()
            for p in range(3):
                head_recv(h, a, p).wait_recv()

        arrive(0)
        arrive(1)

        @pl.when(h == HD - 1)
        def _():
            back_start(0, BACK_ONE)

        scores(h)
        arrive(2)
        weight_grad(h)
        for p in range(3):
            first_x(h, p).start()
            first_z(h, p).start()

        @pl.when(h >= 1)
        def _():
            after_first(h - 1)
            backward(h - 1)
            after_second(h - 1)

    after_first(HD - 1)
    back_start(BACK_ONE, BACK_TWO)
    after_second(HD - 1)

    @pl.loop(0, HD)
    def _(h):
        after_third(h)

    def pack(device):
        tiles = [sums[jnp.clip(slot_from[s, device, 0], 0, HD * 20 - 1)] for s in range(SL)]
        for t in range(4):
            tx[device, t] = jnp.concatenate([tiles[2 * t], tiles[min(2 * t + 1, SL - 1)]], axis=0).astype(BF)

    def to_owner(k):
        device = lax.rem(dp + k, 32)
        return remote(tx.at[device], rx.at[dp // 2], t_send.at[k // 2 - 1], t_recv.at[k // 2 - 1], (device, me))

    @pl.loop(1, 16)
    def _(i):
        pack(lax.rem(dp + 2 * i, 32))
        to_owner(2 * i).start()

    back_start(BACK_TWO, BACK_THREE)
    backward(HD - 1)
    pack(dp)
    rx[dp // 2] = tx[dp]
    for i in range(4):
        state_copy(i).wait()

    @pl.loop(1, 16)
    def _(i):
        to_owner(2 * i).wait_recv()

    def state_out(i):
        return pltpu.make_async_copy(state.at[i], states_out[i], state_out_sem.at[i])

    arrived = rx[...]
    even = None
    for s in range(SL):
        if s % 2 == 0:
            both = arrived[:, s // 2].astype(F32)
        half = both[:, :8] if s % 2 == 0 else both[:, 8:]
        gradient = half.reshape(128, 128) * (1.0 / 32.0)
        before = [state[i, s] for i in range(4)]
        stepped = adam_step(*before, gradient)
        keep = jnp.full((128, 128), slot_from[SL, dp, 0], jnp.int32) > s
        after = [jnp.where(keep, new, old) for new, old in zip(stepped, before)]
        for i in range(4):
            state[i, s] = after[i]
        fresh = after[0].reshape(16, 8, 128)
        if s % 2 == 0:
            even = fresh
        if s % 2 == 1 or s == SL - 1:
            pieces[:, s // 2] = jnp.concatenate([even, fresh], axis=1).astype(BF)
    mine = 4 * x + z

    def from_owner(k):
        device = lax.rem(dp + k, 32)
        return remote(pieces.at[device // 2], landed.at[dp], n_send.at[k - 1], n_recv.at[k - 1], (device, me))

    @pl.loop(0, 31)
    def _(i):
        from_owner(jnp.where(i < 16, 2 * i + 1, 2 * i - 30)).start()

    back_start(BACK_THREE, 3 * HD)
    for i in range(4):
        state_out(i).start()
    landed[dp] = pieces[mine]

    @pl.loop(1, 32)
    def _(k):
        from_owner(k).wait_recv()

    def arrange(pairs):
        for pair in pairs:
            halves = []
            for b in (2 * pair, 2 * pair + 1):
                source = jnp.clip(block_from[0, b], 0, 255)
                tile = landed[source // 8, lax.rem(source, 8) // 2].astype(F32)
                odd = jnp.full((8, 128), lax.rem(source, 2), jnp.int32) == 1
                halves.append(jnp.where(odd, tile[8:], tile[:8]))
            w16[x, z, pair] = jnp.concatenate(halves, axis=0).astype(BF)

    here = ((x, z), (z, x))

    def device_of(f, first, second):
        a, b = (first, second) if f == 0 else (second, first)
        return (dp_index(a, b, yh), me)

    def piece(f, first, second, d, kind):
        start, size = f * 25, 25
        if kind == 1:
            start, size = (start, 12) if d == 0 else (start + 12, 13)
        a, b = (first, second) if f == 0 else (second, first)
        return w16.at[a, b, pl.ds(start, size)]

    ways = (1, 3)

    def ring_one(f, d, kind):
        a, b = here[f]
        place = piece(f, a if kind == 0 else ring(a, ways[1 - d]), b, d, kind)
        return remote(place, place, a_send.at[f, d, kind], a_recv.at[f, d, kind], device_of(f, ring(a, ways[d]), b))

    def landed_one(f, d, kind):
        a, b = here[f]
        place = piece(f, ring(a, ways[1 - d]) if kind == 0 else ring(a, 2), b, d, kind)
        return remote(place, place, a_send.at[f, d, kind], a_recv.at[f, d, kind], device_of(f, ring(a, ways[1 - d]), b))

    def ring_two(f, i, d, kind):
        a, b = here[f]
        place = piece(f, ring(a, i), b if kind == 0 else ring(b, ways[1 - d]), d, kind)
        to = device_of(f, a, ring(b, ways[d]))
        return remote(place, place, b_send.at[f, i, d, kind], b_recv.at[f, i, d, kind], to)

    def landed_two(f, i, d, kind):
        a, b = here[f]
        place = piece(f, ring(a, i), ring(b, ways[1 - d]) if kind == 0 else ring(b, 2), d, kind)
        to = device_of(f, a, ring(b, ways[1 - d]))
        return remote(place, place, b_send.at[f, i, d, kind], b_recv.at[f, i, d, kind], to)

    both = [(f, d) for d in range(2) for f in range(2)]
    for f in range(2):
        arrange(range(f * 25, f * 25 + 25))
        for d in range(2):
            ring_one(f, d, 0).start()
        for d in range(2):
            ring_two(f, 0, d, 0).start()
    for f, d in both:
        landed_one(f, d, 0).wait_recv()
        ring_one(f, d, 1).start()
        for way in range(2):
            ring_two(f, ways[1 - d], way, 0).start()
    for f, d in both:
        landed_two(f, 0, d, 0).wait_recv()
        ring_two(f, 0, d, 1).start()
    for f, d in both:
        landed_one(f, d, 1).wait_recv()
    for f, d in both:
        ring_two(f, 2, d, 0).start()
    for i in (3, 1, 2):
        for f, d in both:
            landed_two(f, i, d, 0).wait_recv()
            ring_two(f, i, d, 1).start()

    def w_copy(h):
        return pltpu.make_async_copy(w_new.at[h], w_out.at[h], w_sem.at[h])

    def rows_of(first, pairs):
        for pair in pairs:
            h, c = pair // 10, pair % 10
            for m in range(2):
                low = w16[first, 2 * m, pair].astype(F32)
                high = w16[first, 2 * m + 1, pair].astype(F32)
                place = pl.ds(pl.multiple_of(first * 32 + m * 16, 16), 16)
                left = jnp.concatenate([low[:8], high[:8]], axis=0)
                right = jnp.concatenate([low[8:], high[8:]], axis=0)
                w_new[h, place, c * 256 : c * 256 + 128] = left.astype(BF)
                w_new[h, place, c * 256 + 128 : c * 256 + 256] = right.astype(BF)

    for i in (0, 3, 1, 2):
        for d in range(2):
            landed_two(0, i, d, 1).wait_recv()
        rows_of(ring(x, i), range(25))
    for h in range(2):
        w_copy(h).start()
    for i in range(4):
        for d in range(2):
            landed_two(1, i, d, 1).wait_recv()

    @pl.loop(0, 4)
    def _(first):
        rows_of(first, range(25, 50))

    for h in range(2, HD):
        w_copy(h).start()

    for c in range(CC):
        cot_cross(c).wait_send()
        cot_forward(c).wait_send()
    cot_sibling().wait_send()

    @pl.loop(0, HD)
    def _(h):
        for p in range(3):
            first_x(h, p).wait_send()
            first_z(h, p).wait_send()
            second_x(h, p).wait_send()
            second_z(h, p).wait_send()
        for a in range(3):
            back_own(h, a).wait()
            for p in range(3):
                head_send(h, a, p).wait_send()
                back_copy(h, a, p).wait_send()
                back_recv_copy(h, a, p).wait_recv()

    for f, d in both:
        for kind in range(2):
            ring_one(f, d, kind).wait_send()
            for i in range(4):
                ring_two(f, i, d, kind).wait_send()

    @pl.loop(1, 32)
    def _(k):
        from_owner(k).wait_send()

    @pl.loop(1, 16)
    def _(i):
        to_owner(2 * i).wait_send()

    @pl.loop(0, HD)
    def _(h):
        other_half(h).wait_send()

    for i in range(4):
        state_out(i).wait()
    for h in range(HD):
        w_copy(h).wait()


def step(q, k, v, cot, w, tile_list, owners, *states):
    any_space = pl.BlockSpec(memory_space=pl.ANY)
    smem = pl.BlockSpec(memory_space=pltpu.SMEM)
    sems = lambda *shape: pltpu.SemaphoreType.DMA(shape)
    return pl.pallas_call(
        step_kernel,
        out_shape=[jax.ShapeDtypeStruct((TOK, OUTW), BF)] * 3 + [jax.ShapeDtypeStruct((HD, 128, OUTW), BF)]
        + [jax.ShapeDtypeStruct((SL, 128, 128), F32)] * 4,
        in_specs=[any_space] * 5 + [smem] * 2 + [any_space] * 4,
        out_specs=[any_space] * 8,
        scratch_shapes=[
            pltpu.VMEM((3, HD, LEN, 128), BF),
            pltpu.VMEM((LEN, OUTW), BF),
            pltpu.VMEM((HD * 128, OUTW), BF),
            pltpu.VMEM((HD, LEN, 128), BF),
            pltpu.VMEM((3, HD, LEN, 128), BF),
            pltpu.VMEM((128, LEN), BF),
            pltpu.VMEM((128, LEN), BF),
            pltpu.VMEM((128, LEN), BF),
            pltpu.VMEM((2, 4, LEN, 256), F32),
            pltpu.VMEM((4, LEN, 256), BF),
            pltpu.VMEM((2, 4, 8, 256), F32),
            pltpu.VMEM((LEN, 128), F32),
            pltpu.VMEM((LEN, 128), F32),
            pltpu.VMEM((HD, 4, 32, 1280), BF),
            pltpu.VMEM((HD, 4, 32, 1280), BF),
            pltpu.VMEM((HD, 3, 32, 1280), BF),
            pltpu.VMEM((HD, 3, 32, 1280), BF),
            pltpu.VMEM((HD, 4, 16, 640), BF),
            pltpu.VMEM((HD, 4, 16, 640), BF),
            pltpu.VMEM((HD, 3, 16, 640), BF),
            pltpu.VMEM((HD, 3, 16, 640), BF),
            pltpu.VMEM((HD * 20, 8, 128), F32),
            sems(2 + 3 * HD),
            sems(HD, 3),
            sems(2 * CC + 1),
            sems(2 * CC + 1),
            *([sems(HD, 3, 3)] * 4),
            *([sems(HD, 3)] * 8),
            pltpu.VMEM((4, SL, 128, 128), F32),
            pltpu.VMEM((32, 4, 16, 128), BF),
            pltpu.VMEM((16, 4, 16, 128), BF),
            pltpu.VMEM((16, 4, 16, 128), BF),
            pltpu.VMEM((32, 4, 16, 128), BF),
            pltpu.VMEM((4, 4, 50, 16, 128), BF),
            sems(4),
            sems(4),
            sems(15),
            sems(15),
            sems(31),
            sems(31),
            sems(2, 2, 2),
            sems(2, 2, 2),
            sems(2, 4, 2, 2),
            sems(2, 4, 2, 2),
            pltpu.VMEM((4, 8, 256), F32),
            pltpu.VMEM((8, 32, 128), jnp.int32),
            pltpu.VMEM((8, 128), jnp.int32),
            pltpu.SMEM((8, 32, 128), jnp.int32),
            pltpu.SMEM((8, 128), jnp.int32),
            sems(2),
            pltpu.VMEM((HD, 128, OUTW), BF),
            sems(HD),
            pltpu.VMEM((HD, 2, 16, 640), F32),
            pltpu.VMEM((HD, 2, 16, 640), BF),
            pltpu.VMEM((HD, 2, 16, 640), BF),
            sems(HD),
            sems(HD),
        ],
        compiler_params=pltpu.CompilerParams(
            collective_id=0, has_side_effects=True, vmem_limit_bytes=56 * 1024 * 1024
        ),
    )(q, k, v, cot, w, tile_list, owners, *states)


def copy_kernel(*refs):
    sources, targets, held, sem = refs[:8], refs[8:16], refs[16:24], refs[24]
    pairs = []
    for source, buffer, target in zip(sources, held, targets):
        half = source.shape[0] // 2
        for part in (pl.ds(0, half), pl.ds(half, source.shape[0] - half)):
            i = len(pairs)
            pairs.append((
                pltpu.make_async_copy(source.at[part], buffer.at[part], sem.at[0, i]),
                pltpu.make_async_copy(buffer.at[part], target.at[part], sem.at[1, i]),
            ))
    for load, _ in pairs:
        load.start()
    for load, store in pairs:
        load.wait()
        store.start()
    for _, store in pairs:
        store.wait()


def copy_out(*arrays):
    space = pl.BlockSpec(memory_space=pltpu.MemorySpace.HBM)
    return pl.pallas_call(
        copy_kernel,
        out_shape=[jax.ShapeDtypeStruct(a.shape, a.dtype) for a in arrays],
        in_specs=[space] * 8,
        out_specs=[space] * 8,
        scratch_shapes=[pltpu.VMEM(a.shape, a.dtype) for a in arrays] + [pltpu.SemaphoreType.DMA((2, 16))],
        compiler_params=pltpu.CompilerParams(vmem_limit_bytes=60 * 1024 * 1024),
    )(*arrays)


def local(q, k, v, cot, w, tile_list, owners, master, one, two, mean):
    results = step(
        q, k, v, cot, w, tile_list, owners[:, 0], master[0], one[0], two[0], mean[0]
    )
    dq, dk, dv, new_w, *states = copy_out(*results)
    return (dq, dk, dv, new_w.reshape(HD * 128, OUTW), *[s[None] for s in states])


def solution(mesh):
    tokens = P(("dp", "seq"), None)
    state = P("dp", "seq", None, None)
    return jax.shard_map(
        local,
        mesh=mesh,
        in_specs=(tokens,) * 4 + (P("seq", None), P(), P()) + (state,) * 4,
        out_specs=(tokens,) * 3 + (P("seq", None),) + (state,) * 4,
        check_vma=False,
    )
```
